512 devices in a mesh: group: 16 (over x, y_lo, core), head: 32 (over z, y_hi).
Axes of the slice: x: 4, y: 4 (y_hi: 2, y_lo: 2; y = y_hi * 2 + y_lo), z: 16, core: 2. Of those that a mesh axis runs over, the one named last changes fastest.
Arguments:
- enc_resid: bfloat16 [1024, 1024], P('group'), may hold values from -6 to 6
- enc_qkv: bfloat16 [3, 1024, 16384], P(None, 'group', 'head'), may hold values from -6 to 6
- enc_bias: float32 [64, 64], replicated, may hold values from -4 to 315
- out_weight: bfloat16 [16384, 1024], P(('head', 'group')), may hold values from -0.046875 to 0.046875
- final_gain: float32 [1024], replicated, may hold values from 0.25 to 1.75
- key_weight: bfloat16 [1024, 16384], P('group', 'head'), may hold values from -0.1875 to 0.1875
- value_weight: bfloat16 [1024, 16384], P('group', 'head'), may hold values from -0.1875 to 0.1875
- dec_query: bfloat16 [6144, 16384], P('group', 'head'), may hold values from -6 to 6
- cross_bias: float32 [384, 64], replicated, may hold values from -4 to 315
- out_grad: bfloat16 [6144, 16384], P('group', 'head'), may hold values from -6 to 6
- sources: int32 [16, 3], replicated, may hold values from 0 to 15, all different within a row
- head_keep: int32 [16, 128], P('group', 'head'), may hold values 0 or 1
Outputs:
- context: bfloat16 [6144, 16384], P('group', 'head')
- memory_grad: bfloat16 [1024, 1024], P('group')
The draws below stay inside these ranges and needn't reach their ends.
Inputs may be any that keep to these rules, and one draw needn't show every extreme that they name: `sources`: each row names 3 different encoder groups; every encoder group is named by some row.
All inputs are finite; a program needn't handle non-finite values. No bound on the sum of `head_keep` on one device may be relied on, other than what follows from the above.
Results may differ from the reference program's by a relative error of at most 0.034.
Values may be sent and summed in bfloat16 or wider, within the bound.
A program may use at most 64 MiB of HBM per device.

```python
import math
import jax
import jax.numpy as jnp
from jax import lax

D = 1024
HEADS = 128
DK = 128
SEQ = 64
QROWS = 384
MEM = 3
INNER = 16384
ENC_ROWS = 1024
DEC_ROWS = 6144
N_GROUP = 16


def biased_rows(key, rows, cols):
    first = jax.random.fold_in(key, 0)
    base = jax.random.truncated_normal(first, -4.0, 4.0, (rows, cols), jnp.float32)
    return base


def draw_enc_bias(key, part):
    return biased_rows(jax.random.fold_in(key, 11), SEQ, SEQ)


def draw_cross_bias(key, part):
    return biased_rows(jax.random.fold_in(key, 23), QROWS, SEQ)


def touch_ends(result, stream_key, smallest, high):
    index_at = [jax.random.randint(jax.random.fold_in(stream_key, axis), (), 0, length) for axis, length in enumerate(result.shape)]
    longest = result.shape.index(max(result.shape))
    next_to = index_at[:longest] + [(index_at[longest] + 1) % result.shape[longest]] + index_at[longest + 1:]
    return result.at[tuple(index_at)].set(smallest).at[tuple(next_to)].set(high)


def block_levels(stream_key, dims, pieces, least, high):
    gain = 1.0
    for position, blocks in pieces:
        draws = jax.random.uniform(jax.random.fold_in(jax.random.fold_in(stream_key, 6), position), (blocks,), jnp.float32, least / len(pieces), high / len(pieces))
        gain = gain * jnp.repeat(jnp.exp(draws), dims[position] // blocks).reshape((-1,) + (1,) * (len(dims) - 1 - position))
    return gain


def picks_of(rng, rows, number_of, top, lift):
    order = jax.random.permutation(jax.random.fold_in(rng, 1), number_of)
    pull = order
    for power in range(3):
        pull = pull * pull // number_of
    pull = pull * lift // number_of
    lots = jax.random.randint(jax.random.fold_in(rng, 2), (rows, number_of), 0, 4096) + pull
    sure = jax.random.permutation(jax.random.fold_in(rng, 3), rows)[jnp.arange(number_of) % rows]
    lots = jnp.where(jnp.arange(rows)[:, None] == sure[None, :], 1 << 14, lots)
    merit = lots * number_of + jnp.arange(number_of)
    return lax.top_k(merit.astype(jnp.int32), top)[1].astype(jnp.int32)


def scatter_about(key, shape, spread, bound, cuts=(), kind=jnp.bfloat16):
    result = spread * jax.random.normal(key, shape, jnp.float32)
    if cuts:
        result = result * block_levels(key, shape, cuts, -0.22, 0.18)
    return jnp.clip(result, -bound, bound).astype(kind)


def setup_inputs(seed: int = 0) -> dict:
    key_of = jax.random.split(jax.random.key(seed), 13)
    enc_resid = scatter_about(key_of[0], (ENC_ROWS, D), 1.0, 6.0, ((0, 16),))
    enc_qkv = scatter_about(key_of[1], (3, ENC_ROWS, INNER), 1.0, 6.0, ((1, 16), (2, 32)))
    enc_bias = draw_enc_bias(jax.random.fold_in(key_of[12], 71), 0)
    out_weight = scatter_about(key_of[3], (INNER, D), INNER ** -0.5, 0.046875, ((0, 512),))
    final_gain = jnp.clip(1.0 + 0.15 * jax.random.normal(key_of[4], (D,), jnp.float32), 0.25, 1.75)
    key_weight = scatter_about(key_of[5], (D, INNER), D ** -0.5, 0.1875, ((0, 16), (1, 32)))
    value_weight = scatter_about(key_of[6], (D, INNER), D ** -0.5, 0.1875, ((0, 16), (1, 32)))
    dec_query = scatter_about(key_of[7], (DEC_ROWS, INNER), 1.0, 6.0, ((0, 16), (1, 32)))
    cross_bias = draw_cross_bias(jax.random.fold_in(key_of[12], 71), 0)
    out_grad = scatter_about(key_of[9], (DEC_ROWS, INNER), 1.0, 6.0, ((0, 16), (1, 32)))
    sources = picks_of(key_of[10], N_GROUP, N_GROUP, MEM, 3072)
    head_keep = touch_ends((jax.random.randint(key_of[11], (N_GROUP, HEADS), 0, 4) < 3).astype(jnp.int32), jax.random.fold_in(key_of[11], 1), 0, 1)
    return {"enc_resid": enc_resid, "enc_qkv": enc_qkv, "enc_bias": enc_bias, "out_weight": out_weight, "final_gain": final_gain, "key_weight": key_weight, "value_weight": value_weight, "dec_query": dec_query, "cross_bias": cross_bias, "out_grad": out_grad, "sources": sources, "head_keep": head_keep}


def softmax_rows(scores):
    top = lax.optimization_barrier(jnp.max(scores, axis=-1, keepdims=True))
    expd = jnp.exp(scores - top)
    return expd / lax.optimization_barrier(jnp.sum(expd, axis=-1, keepdims=True))

def reference(enc_resid, enc_qkv, enc_bias, out_weight, final_gain, key_weight, value_weight, dec_query, cross_bias, out_grad, sources, head_keep):
    scale = 1.0 / math.sqrt(DK)
    fq = enc_qkv[0].astype(jnp.float32).reshape(N_GROUP, SEQ, HEADS, DK)
    fk = enc_qkv[1].astype(jnp.float32).reshape(N_GROUP, SEQ, HEADS, DK)
    fv = enc_qkv[2].astype(jnp.float32).reshape(N_GROUP, SEQ, HEADS, DK)
    enc_scores = jnp.einsum('gqhd,gkhd->ghqk', fq, fk) * scale + enc_bias
    enc_prob = softmax_rows(enc_scores).astype(jnp.bfloat16)
    enc_ctx = jnp.einsum('ghqk,gkhd->gqhd', enc_prob.astype(jnp.float32), fv).astype(jnp.bfloat16)
    enc_ctx = enc_ctx.reshape(ENC_ROWS, INNER)
    memory = enc_resid.astype(jnp.float32) + jnp.dot(enc_ctx, out_weight, preferred_element_type=jnp.float32)
    inv = lax.rsqrt(lax.optimization_barrier(jnp.mean(memory * memory, axis=-1, keepdims=True)) + 1e-06)
    mem_norm = (memory * inv * final_gain).astype(jnp.bfloat16)
    keys = jnp.dot(mem_norm, key_weight, preferred_element_type=jnp.float32).astype(jnp.bfloat16)
    values = jnp.dot(mem_norm, value_weight, preferred_element_type=jnp.float32).astype(jnp.bfloat16)
    keys4 = keys.reshape(N_GROUP, SEQ, HEADS, DK)
    values4 = values.reshape(N_GROUP, SEQ, HEADS, DK)
    queries = dec_query.reshape(N_GROUP, QROWS, HEADS, DK)
    grads = out_grad.reshape(N_GROUP, QROWS, HEADS, DK)
    keeps = head_keep.astype(jnp.float32)
    bias_all = jnp.tile(cross_bias, (1, MEM))

    def decode(carry, item):
        dk_total, dv_total = carry
        query, grad_in, keep_row, src = item
        mk = keys4[src].reshape(MEM * SEQ, HEADS, DK).astype(jnp.float32)
        mv = values4[src].reshape(MEM * SEQ, HEADS, DK).astype(jnp.float32)
        fquery = query.astype(jnp.float32)
        cross = jnp.einsum('qhd,khd->hqk', fquery, mk) * scale + bias_all
        prob = softmax_rows(cross)
        prob_low = prob.astype(jnp.bfloat16)
        attn = jnp.einsum('hqk,khd->qhd', prob_low.astype(jnp.float32), mv)
        ctx = (attn * keep_row[None, :, None]).astype(jnp.bfloat16)
        grad = (grad_in.astype(jnp.float32) * keep_row[None, :, None]).astype(jnp.bfloat16)
        fgrad = grad.astype(jnp.float32)
        dprob = jnp.einsum('qhd,khd->hqk', fgrad, mv)
        delta = lax.optimization_barrier(jnp.sum(prob * dprob, axis=-1, keepdims=True))
        dscore = (prob * (dprob - delta) * scale).astype(jnp.bfloat16)
        dk_part = jnp.einsum('hqk,qhd->khd', dscore.astype(jnp.float32), fquery).astype(jnp.bfloat16)
        dv_part = jnp.einsum('hqk,qhd->khd', prob_low.astype(jnp.float32), fgrad).astype(jnp.bfloat16)
        dk_part = lax.optimization_barrier(dk_part).astype(jnp.float32).reshape(MEM, SEQ, INNER)
        dv_part = lax.optimization_barrier(dv_part).astype(jnp.float32).reshape(MEM, SEQ, INNER)
        dk_total = dk_total.at[src].add(dk_part)
        dv_total = dv_total.at[src].add(dv_part)
        return ((dk_total, dv_total), ctx)
    start = (jnp.zeros((N_GROUP, SEQ, INNER), jnp.float32), jnp.zeros((N_GROUP, SEQ, INNER), jnp.float32))
    (dk_total, dv_total), contexts = lax.scan(decode, start, (queries, grads, keeps, sources.astype(jnp.int32)))
    context = contexts.reshape(DEC_ROWS, INNER)
    dkeys = dk_total.astype(jnp.bfloat16).reshape(ENC_ROWS, INNER)
    dvalues = dv_total.astype(jnp.bfloat16).reshape(ENC_ROWS, INNER)
    dnorm = jnp.dot(dkeys, key_weight.T, preferred_element_type=jnp.float32) + jnp.dot(dvalues, value_weight.T, preferred_element_type=jnp.float32)
    normed = memory * inv
    scaled = dnorm * final_gain
    memory_grad = (inv * (scaled - normed * lax.optimization_barrier(jnp.mean(scaled * normed, axis=-1, keepdims=True)))).astype(jnp.bfloat16)
    return (context, memory_grad)
```

```python
import functools
import math

import jax
import jax.numpy as jnp
from jax import lax
from jax.experimental import pallas as pl
from jax.experimental.pallas import tpu as pltpu
from jax.sharding import PartitionSpec as P

MESH = pl.DeviceIdType.MESH
BF16 = jnp.bfloat16
F32 = jnp.float32
DK = 128
LANES = 128
EPS = 1e-06


def mm(a, b, ca, cb):
    return lax.dot_general(a, b, (((ca,), (cb,)), ((), ())), preferred_element_type=F32)


def kernel(
    ngroup,
    nhead,
    mem,
    sources,
    keep,
    resid,
    qkv,
    enc_bias,
    gain,
    cross_bias,
    out_w,
    key_w,
    value_w,
    query_hbm,
    grad_hbm,
    context_hbm,
    memory_grad,
    wo,
    kw,
    vw,
    query,
    grad,
    context,
    flat,
    resid_flat,
    out_send,
    out_recv,
    norm_all,
    norm_pick,
    dn_send,
    dn_recv,
    dn_all,
    mg_all,
    local_sem,
    context_sem,
    wo_send,
    wo_recv,
    wo_pass_send,
    wo_pass_recv,
    kv_send,
    kv_recv,
    kv_pass_send,
    kv_pass_recv,
    phase_send,
    phase_recv,
):
    seq, dim = resid.shape
    width = query.shape[1]
    nheads = width // DK
    chunks = dim // LANES
    own_rows = seq // nhead
    blk = own_rows * chunks
    scale = 1.0 / math.sqrt(DK)
    g = lax.axis_index("group")
    h = lax.axis_index("head")
    core = lax.rem(g, 2)
    chip = lax.div(g, 2)
    sibling = g + 1 - 2 * core
    nchip = ngroup // 2

    def each(n, body):
        lax.fori_loop(1, n, lambda k, c: (body(k), c)[1], 0)

    def group_peer(k):
        return lax.rem(g + k, ngroup)

    def head_peer(k):
        return lax.rem(h + k, nhead)

    def remote(src, dst, send, recv, where):
        return pltpu.make_async_remote_copy(
            src_ref=src,
            dst_ref=dst,
            send_sem=send,
            recv_sem=recv,
            device_id=where,
            device_id_type=MESH,
        )

    def total(ref, send, recv):
        return remote(ref, ref, send, recv, {"group": sibling})

    barrier = pltpu.get_barrier_semaphore()
    each(ngroup, lambda k: pl.semaphore_signal(barrier, inc=1, device_id={"group": group_peer(k)}, device_id_type=MESH))
    each(nhead, lambda k: pl.semaphore_signal(barrier, inc=1, device_id={"head": head_peer(k)}, device_id_type=MESH))
    locals_ = [
        pltpu.make_async_copy(query_hbm, query, local_sem.at[0]),
        pltpu.make_async_copy(grad_hbm, grad, local_sem.at[1]),
        pltpu.make_async_copy(out_w, wo.at[g], local_sem.at[2]),
        pltpu.make_async_copy(key_w, kw.at[g], local_sem.at[3]),
        pltpu.make_async_copy(value_w, vw.at[g], local_sem.at[4]),
    ]
    for copy in locals_:
        copy.start()
    pl.semaphore_wait(barrier, ngroup + nhead - 2)

    def far_group(k):
        return lax.rem(chip + k, nchip) * 2 + core

    def from_group(k):
        return lax.rem(chip - k + nchip, nchip) * 2 + core

    def send_out_weight(k):
        remote(out_w, wo.at[g], wo_send, wo_recv.at[k], {"group": far_group(k)}).start()

    each(nchip, send_out_weight)
    remote(out_w, wo.at[g], wo_pass_send, wo_pass_recv, {"group": sibling}).start()

    bias = enc_bias[...]
    ctx = []
    for n in range(nheads):
        cols = slice(n * DK, (n + 1) * DK)
        scores = mm(qkv[0, :, cols], qkv[1, :, cols], 1, 1) * scale + bias
        e = jnp.exp(scores - jnp.max(scores, axis=1, keepdims=True))
        p = (e * (1.0 / jnp.sum(e, axis=1, keepdims=True))).astype(BF16)
        ctx.append(mm(p, qkv[2, :, cols], 1, 0).astype(BF16))
    ctx = jnp.concatenate(ctx, axis=1)

    def to_flat(x, ref, base):
        rows = x.shape[0]
        for c in range(chunks):
            ref[pl.ds(base * chunks + c, rows, stride=chunks), :] = x[:, c * LANES : (c + 1) * LANES]

    def from_flat(ref, base, rows, c):
        return ref[pl.ds(base * chunks + c, rows, stride=chunks), :]

    to_flat(resid[...].astype(F32), resid_flat, 0)

    def pass_out_weight(k):
        there = wo.at[from_group(k)]
        remote(there, there, wo_send, wo_recv.at[k], {"group": sibling}).wait_recv()
        remote(there, there, wo_pass_send, wo_pass_recv, {"group": sibling}).start()

    each(nchip, pass_out_weight)
    locals_[2].wait()
    total(wo.at[pl.ds(0, nchip)], wo_pass_send, wo_pass_recv).wait_recv()
    part = mm(ctx, wo[...].reshape(width, dim), 1, 0)

    to_flat(part, flat, 0)
    out_send[...] = flat[pl.ds(0, seq * chunks), :].reshape(nhead, blk, LANES).astype(BF16)

    def send_out(k):
        there = head_peer(k)
        remote(out_send.at[there], out_recv.at[k - 1], phase_send.at[0], phase_recv.at[0], {"head": there}).start()

    each(nhead, send_out)

    def send_kv(k):
        where = {"group": far_group(k)}
        remote(key_w, kw.at[g], kv_send, kv_recv.at[0, k], where).start()
        remote(value_w, vw.at[g], kv_send, kv_recv.at[1, k], where).start()

    each(nchip, send_kv)
    remote(key_w, kw.at[g], kv_pass_send, kv_pass_recv, {"group": sibling}).start()
    remote(value_w, vw.at[g], kv_pass_send, kv_pass_recv, {"group": sibling}).start()

    mine = pl.ds(pl.multiple_of(h * blk, blk), blk)
    memory = flat[mine, :] + resid_flat[mine, :]
    total(out_recv, phase_send.at[0], phase_recv.at[0]).wait_recv()
    memory = memory + jnp.sum(out_recv[...].astype(F32), axis=0)

    def row_mean(x):
        x3 = x.reshape(own_rows, chunks, LANES)
        m = jnp.sum(jnp.sum(x3, axis=1, keepdims=True), axis=2, keepdims=True) * (1.0 / dim)
        return jnp.broadcast_to(m, x3.shape).reshape(blk, LANES)

    gains = jnp.broadcast_to(gain[...][None], (own_rows, chunks, LANES)).reshape(blk, LANES)
    inv = lax.rsqrt(row_mean(memory * memory) + EPS)
    normed = memory * inv
    norm_all[g] = (normed * gains).astype(BF16)

    def send_norm(k):
        there = norm_all.at[g]
        remote(there, there, phase_send.at[1], phase_recv.at[1], {"group": group_peer(k)}).start()

    each(ngroup, send_norm)
    total(norm_all.at[pl.ds(0, ngroup - 1)], phase_send.at[1], phase_recv.at[1]).wait_recv()

    for s in range(mem):
        norm_pick[h, s * blk : (s + 1) * blk, :] = norm_all[sources[g, s]]

    def send_pick(k):
        there = norm_pick.at[h]
        remote(there, there, phase_send.at[2], phase_recv.at[2], {"head": head_peer(k)}).start()

    each(nhead, send_pick)

    def pass_kv(k):
        for i, ref in ((0, kw), (1, vw)):
            there = ref.at[from_group(k)]
            remote(there, there, kv_send, kv_recv.at[i, k], {"group": sibling}).wait_recv()
            remote(there, there, kv_pass_send, kv_pass_recv, {"group": sibling}).start()

    each(nchip, pass_kv)
    for i in (0, 1, 3, 4):
        locals_[i].wait()
    total(kw.at[pl.ds(0, 2 * nchip)], kv_pass_send, kv_pass_recv).wait_recv()
    total(norm_pick.at[pl.ds(0, nhead - 1)], phase_send.at[2], phase_recv.at[2]).wait_recv()
    for s in range(mem):
        rows = norm_pick[:, s * blk : (s + 1) * blk, :].astype(F32).reshape(seq * chunks, LANES)
        flat[pl.ds(s * seq * chunks, seq * chunks), :] = rows
    rows = mem * seq
    picked = jnp.concatenate([from_flat(flat, 0, rows, c).astype(BF16) for c in range(chunks)], axis=1)

    key_full = kw[...].reshape(dim, width)
    value_full = vw[...].reshape(dim, width)
    keys = mm(picked, key_full, 1, 0).astype(BF16)
    values = mm(picked, value_full, 1, 0).astype(BF16)
    cbias = cross_bias[...]
    qrows = query.shape[0]
    dks, dvs = [], []
    for n in range(nheads):
        cols = slice(n * DK, (n + 1) * DK)
        kept = keep[0, n].astype(F32)
        q_n, g_n = query[:, cols], grad[:, cols]
        k_n, v_n = keys[:, cols], values[:, cols]
        cross = (mm(k_n, q_n, 1, 1) * scale).reshape(mem, seq, qrows) + cbias[None]
        cross = cross.reshape(rows, qrows)
        e = jnp.exp(cross - jnp.max(cross, axis=0, keepdims=True))
        prob = e * (1.0 / jnp.sum(e, axis=0, keepdims=True))
        prob_low = prob.astype(BF16)
        context[:, cols] = (mm(prob_low, v_n, 0, 0) * kept).astype(BF16)
        dprob = mm(v_n, g_n, 1, 1)
        delta = jnp.sum(prob * dprob, axis=0, keepdims=True)
        dscore = (prob * (dprob - delta) * (scale * kept)).astype(BF16)
        dks.append(mm(dscore, q_n, 1, 0).astype(BF16))
        dvs.append((mm(prob_low, g_n, 1, 0) * kept).astype(BF16))
    context_copy = pltpu.make_async_copy(context, context_hbm, context_sem)
    context_copy.start()
    dks = jnp.concatenate(dks, axis=1)
    dvs = jnp.concatenate(dvs, axis=1)
    dnorm = mm(dks, key_full, 1, 1) + mm(dvs, value_full, 1, 1)

    to_flat(dnorm, flat, 0)
    for s in range(mem):
        block = flat[pl.ds(s * seq * chunks, seq * chunks), :].reshape(nhead, blk, LANES)
        dn_send[:, s * blk : (s + 1) * blk, :] = block.astype(BF16)

    def send_dn(k):
        there = head_peer(k)
        remote(dn_send.at[there], dn_recv.at[k - 1], phase_send.at[3], phase_recv.at[3], {"head": there}).start()

    each(nhead, send_dn)
    own = [flat[pl.ds(pl.multiple_of(s * seq * chunks + h * blk, blk), blk), :] for s in range(mem)]
    total(dn_recv, phase_send.at[3], phase_recv.at[3]).wait_recv()
    dn_all[g] = (jnp.concatenate(own, axis=0) + jnp.sum(dn_recv[...].astype(F32), axis=0)).astype(BF16)

    def send_all(k):
        there = dn_all.at[g]
        remote(there, there, phase_send.at[4], phase_recv.at[4], {"group": group_peer(k)}).start()

    each(ngroup, send_all)
    total(dn_all.at[pl.ds(0, ngroup - 1)], phase_send.at[4], phase_recv.at[4]).wait_recv()
    acc = jnp.zeros((blk, LANES), F32)
    for d in range(ngroup):
        for s in range(mem):
            block = dn_all[d, s * blk : (s + 1) * blk, :].astype(F32)
            acc = acc + block * (sources[d, s] == g).astype(F32)
    scaled = acc * gains
    mg_all[h] = (inv * (scaled - normed * row_mean(scaled * normed))).astype(BF16)

    def send_mg(k):
        there = mg_all.at[h]
        remote(there, there, phase_send.at[5], phase_recv.at[5], {"head": head_peer(k)}).start()

    each(nhead, send_mg)
    total(mg_all.at[pl.ds(0, nhead - 1)], phase_send.at[5], phase_recv.at[5]).wait_recv()
    flat[pl.ds(0, seq * chunks), :] = mg_all[...].astype(F32).reshape(seq * chunks, LANES)
    for c in range(chunks):
        memory_grad[:, c * LANES : (c + 1) * LANES] = from_flat(flat, 0, seq, c).astype(BF16)

    context_copy.wait()
    total(wo.at[pl.ds(0, nchip - 1)], wo_send, wo_recv.at[0]).wait_send()
    total(wo.at[pl.ds(0, nchip)], wo_pass_send, wo_pass_recv).wait_send()
    total(kw.at[pl.ds(0, 2 * nchip - 2)], kv_send, kv_recv.at[0, 0]).wait_send()
    total(kw.at[pl.ds(0, 2 * nchip)], kv_pass_send, kv_pass_recv).wait_send()
    for i, ref in enumerate((out_recv, norm_all.at[pl.ds(0, ngroup - 1)], norm_pick.at[pl.ds(0, nhead - 1)], dn_recv, dn_all.at[pl.ds(0, ngroup - 1)], mg_all.at[pl.ds(0, nhead - 1)])):
        total(ref, phase_send.at[i], phase_recv.at[i]).wait_send()


def shards(
    ngroup,
    nhead,
    enc_resid,
    enc_qkv,
    enc_bias,
    out_weight,
    final_gain,
    key_weight,
    value_weight,
    dec_query,
    cross_bias,
    out_grad,
    sources,
    head_keep,
):
    seq, dim = enc_resid.shape
    qrows, width = dec_query.shape
    mem = sources.shape[1]
    chunks = dim // LANES
    blk = seq // nhead * chunks
    nchip = ngroup // 2
    vmem = pl.BlockSpec(memory_space=pltpu.VMEM)
    smem = pl.BlockSpec(memory_space=pltpu.SMEM)
    anyw = pl.BlockSpec(memory_space=pl.ANY)
    dma = pltpu.SemaphoreType.DMA
    return tuple(
        pl.pallas_call(
            functools.partial(kernel, ngroup, nhead, mem),
            out_shape=(
                jax.ShapeDtypeStruct((qrows, width), BF16),
                jax.ShapeDtypeStruct((seq, dim), BF16),
            ),
            in_specs=[smem, smem, vmem, vmem, vmem, vmem, vmem, anyw, anyw, anyw, anyw, anyw],
            out_specs=(anyw, vmem),
            scratch_shapes=[
                pltpu.VMEM((ngroup,) + out_weight.shape, BF16),
                pltpu.VMEM((ngroup,) + key_weight.shape, BF16),
                pltpu.VMEM((ngroup,) + value_weight.shape, BF16),
                pltpu.VMEM((qrows, width), BF16),
                pltpu.VMEM((qrows, width), BF16),
                pltpu.VMEM((qrows, width), BF16),
                pltpu.VMEM((mem * seq * chunks, LANES), F32),
                pltpu.VMEM((seq * chunks, LANES), F32),
                pltpu.VMEM((nhead, blk, LANES), BF16),
                pltpu.VMEM((nhead - 1, blk, LANES), BF16),
                pltpu.VMEM((ngroup, blk, LANES), BF16),
                pltpu.VMEM((nhead, mem * blk, LANES), BF16),
                pltpu.VMEM((nhead, mem * blk, LANES), BF16),
                pltpu.VMEM((nhead - 1, mem * blk, LANES), BF16),
                pltpu.VMEM((ngroup, mem * blk, LANES), BF16),
                pltpu.VMEM((nhead, blk, LANES), BF16),
                dma((5,)),
                dma,
                dma,
                dma((nchip,)),
                dma,
                dma,
                dma,
                dma((2, nchip)),
                dma,
                dma,
                dma((6,)),
                dma((6,)),
            ],
            compiler_params=pltpu.CompilerParams(
                collective_id=0, has_side_effects=True, vmem_limit_bytes=40 * 1024 * 1024
            ),
        )(
            sources,
            head_keep,
            enc_resid,
            enc_qkv,
            enc_bias,
            final_gain.reshape(chunks, LANES),
            cross_bias.T,
            out_weight,
            key_weight,
            value_weight,
            dec_query,
            out_grad,
        )
    )


def solution(mesh):
    in_specs = (
        P("group", None),
        P(None, "group", "head"),
        P(),
        P(("head", "group"), None),
        P(),
        P("group", "head"),
        P("group", "head"),
        P("group", "head"),
        P(),
        P("group", "head"),
        P(),
        P("group", "head"),
    )
    out_specs = (P("group", "head"), P("group", None))
    step = functools.partial(shards, mesh.shape["group"], mesh.shape["head"])
    return jax.shard_map(step, mesh=mesh, in_specs=in_specs, out_specs=out_specs, check_vma=False)
```

```python
import functools
import math

import jax
import jax.numpy as jnp
from jax import lax
from jax.experimental import pallas as pl
from jax.experimental.pallas import tpu as pltpu
from jax.sharding import PartitionSpec as P

MESH = pl.DeviceIdType.MESH
BF16 = jnp.bfloat16
F32 = jnp.float32
DK = 128
LANES = 128
EPS = 1e-06


def mm(a, b, ca, cb):
    return lax.dot_general(a, b, (((ca,), (cb,)), ((), ())), preferred_element_type=F32)


def kernel(
    ngroup,
    nhead,
    mem,
    sources_hbm,
    keep_hbm,
    resid_hbm,
    qkv_hbm,
    enc_bias_hbm,
    gain_hbm,
    cross_bias_hbm,
    out_w,
    key_w,
    value_w,
    query_hbm,
    grad_hbm,
    context,
    memory_grad,
    sources,
    keep,
    resid,
    qkv,
    enc_bias,
    gain,
    cross_bias,
    wo,
    kw,
    vw,
    query,
    grad,
    flat,
    resid_flat,
    out_send,
    out_recv,
    norm_all,
    norm_pick,
    dn_send,
    dn_near,
    dn_sum,
    dn_far,
    dn_all,
    mg_all,
    local_sem,
    wo_send,
    wo_recv,
    wo_pass_send,
    wo_pass_recv,
    kv_send,
    kv_recv,
    kv_pass_send,
    kv_pass_recv,
    far_recv,
    near_recv,
    phase_send,
    phase_recv,
):
    seq, dim = resid.shape
    width = query.shape[1]
    nheads = width // DK
    chunks = dim // LANES
    own_rows = seq // nhead
    blk = own_rows * chunks
    scale = 1.0 / math.sqrt(DK)
    g = lax.axis_index("group")
    h = lax.axis_index("head")
    core = lax.rem(g, 2)
    chip = lax.div(g, 2)
    sibling = g + 1 - 2 * core
    nchip = ngroup // 2

    nz, nx = nhead // 2, ngroup // 4
    z, y = lax.div(h, 2), lax.rem(h, 2)
    gx, gy = lax.div(g, 4), lax.rem(lax.div(g, 2), 2)

    def each(n, body):
        lax.fori_loop(1, n, lambda k, c: (body(k), c)[1], 0)

    def head_at(dz, dy):
        return lax.rem(z + dz + nz, nz) * 2 + lax.rem(y + dy, 2)

    def group_at(dx, dy, dc):
        return lax.rem(gx + dx, nx) * 4 + lax.rem(gy + dy, 2) * 2 + lax.rem(core + dc, 2)

    def head_peer(k):
        j = lax.div(k - 1, 2)
        away = nz // 2 - lax.div(j + 1, 2)
        return head_at(away * (2 * lax.rem(j, 2) - 1), lax.rem(k, 2))

    def spread(dx, dy, dc):
        return -(min(dx, nx - dx) * 4 + dy * 4 + dc)

    steps = [(dx, dy, dc) for dx in range(nx) for dy in range(2) for dc in range(2)][1:]
    group_steps = sorted(steps, key=lambda t: spread(*t))
    chip_steps = [(dx, dy) for dx, dy, dc in group_steps if dc == 0]
    far_steps = sorted(range(2, nz, 4), key=lambda a: -min(a, nz - a))
    near_steps = [(2, 1), (1, 1), (nz - 1, 1), (0, 1), (2, 0), (1, 0), (nz - 1, 0)]

    def remote(src, dst, send, recv, where):
        return pltpu.make_async_remote_copy(
            src_ref=src,
            dst_ref=dst,
            send_sem=send,
            recv_sem=recv,
            device_id=where,
            device_id_type=MESH,
        )

    def total(ref, send, recv):
        return remote(ref, ref, send, recv, {"group": sibling})

    barrier = pltpu.get_barrier_semaphore()
    each(ngroup, lambda k: pl.semaphore_signal(barrier, inc=1, device_id={"group": lax.rem(g + k, ngroup)}, device_id_type=MESH))
    each(nhead, lambda k: pl.semaphore_signal(barrier, inc=1, device_id={"head": head_peer(k)}, device_id_type=MESH))
    locals_ = [
        pltpu.make_async_copy(query_hbm, query, local_sem.at[0]),
        pltpu.make_async_copy(grad_hbm, grad, local_sem.at[1]),
        pltpu.make_async_copy(out_w, wo.at[g], local_sem.at[2]),
        pltpu.make_async_copy(key_w, kw.at[g], local_sem.at[3]),
        pltpu.make_async_copy(value_w, vw.at[g], local_sem.at[4]),
        pltpu.make_async_copy(qkv_hbm, qkv, local_sem.at[5]),
        pltpu.make_async_copy(enc_bias_hbm, enc_bias, local_sem.at[6]),
        pltpu.make_async_copy(resid_hbm, resid, local_sem.at[7]),
        pltpu.make_async_copy(gain_hbm, gain, local_sem.at[8]),
        pltpu.make_async_copy(cross_bias_hbm, cross_bias, local_sem.at[9]),
        pltpu.make_async_copy(sources_hbm, sources, local_sem.at[10]),
        pltpu.make_async_copy(keep_hbm, keep, local_sem.at[11]),
    ]
    for copy in locals_:
        copy.start()
    pl.semaphore_wait(barrier, ngroup + nhead - 2)

    for i, (dx, dy) in enumerate(chip_steps):
        remote(out_w, wo.at[g], wo_send, wo_recv.at[i], {"group": group_at(dx, dy, 0)}).start()
    remote(out_w, wo.at[g], wo_pass_send, wo_pass_recv, {"group": sibling}).start()

    locals_[5].wait()
    locals_[6].wait()
    bias = enc_bias[...]
    ctx = []
    for n in range(nheads):
        cols = slice(n * DK, (n + 1) * DK)
        scores = mm(qkv[0, :, cols], qkv[1, :, cols], 1, 1) * scale + bias
        e = jnp.exp(scores - jnp.max(scores, axis=1, keepdims=True))
        p = (e * (1.0 / jnp.sum(e, axis=1, keepdims=True))).astype(BF16)
        ctx.append(mm(p, qkv[2, :, cols], 1, 0).astype(BF16))
    ctx = jnp.concatenate(ctx, axis=1)

    def to_flat(x, ref, base):
        rows = x.shape[0]
        for c in range(chunks):
            ref[pl.ds(base * chunks + c, rows, stride=chunks), :] = x[:, c * LANES : (c + 1) * LANES]

    def from_flat(ref, base, rows, c):
        return ref[pl.ds(base * chunks + c, rows, stride=chunks), :]

    locals_[7].wait()
    to_flat(resid[...].astype(F32), resid_flat, 0)

    for i, (dx, dy) in enumerate(chip_steps):
        there = wo.at[group_at(nx - dx, dy, 0)]
        remote(there, there, wo_send, wo_recv.at[i], {"group": sibling}).wait_recv()
        remote(there, there, wo_pass_send, wo_pass_recv, {"group": sibling}).start()
    locals_[2].wait()
    total(wo.at[pl.ds(0, nchip)], wo_pass_send, wo_pass_recv).wait_recv()
    part = mm(ctx, wo[...].reshape(width, dim), 1, 0)

    to_flat(part, flat, 0)
    out_send[...] = flat[pl.ds(0, seq * chunks), :].reshape(nhead, blk, LANES).astype(BF16)

    def send_out(k):
        there = head_peer(k)
        remote(out_send.at[there], out_recv.at[k - 1], phase_send.at[0], phase_recv.at[0], {"head": there}).start()

    each(nhead, send_out)

    for i, (dx, dy) in enumerate(chip_steps):
        where = {"group": group_at(dx, dy, 0)}
        remote(key_w, kw.at[g], kv_send, kv_recv.at[0, i], where).start()
        remote(value_w, vw.at[g], kv_send, kv_recv.at[1, i], where).start()
    remote(key_w, kw.at[g], kv_pass_send, kv_pass_recv, {"group": sibling}).start()
    remote(value_w, vw.at[g], kv_pass_send, kv_pass_recv, {"group": sibling}).start()

    mine = pl.ds(pl.multiple_of(h * blk, blk), blk)
    memory = flat[mine, :] + resid_flat[mine, :]
    total(out_recv, phase_send.at[0], phase_recv.at[0]).wait_recv()
    memory = memory + jnp.sum(out_recv[...].astype(F32), axis=0)

    def row_mean(x):
        x3 = x.reshape(own_rows, chunks, LANES)
        m = jnp.sum(jnp.sum(x3, axis=1, keepdims=True), axis=2, keepdims=True) * (1.0 / dim)
        return jnp.broadcast_to(m, x3.shape).reshape(blk, LANES)

    locals_[8].wait()
    gains = jnp.broadcast_to(gain[...][None], (own_rows, chunks, LANES)).reshape(blk, LANES)
    inv = lax.rsqrt(row_mean(memory * memory) + EPS)
    normed = memory * inv
    norm_all[g] = (normed * gains).astype(BF16)

    there = norm_all.at[g]
    for step in group_steps:
        remote(there, there, phase_send.at[1], phase_recv.at[1], {"group": group_at(*step)}).start()
    total(norm_all.at[pl.ds(0, ngroup - 1)], phase_send.at[1], phase_recv.at[1]).wait_recv()

    locals_[10].wait()
    for s in range(mem):
        norm_pick[h, s * blk : (s + 1) * blk, :] = norm_all[sources[s, g]]

    there = norm_pick.at[h]
    for i, a in enumerate(far_steps):
        remote(there, there, phase_send.at[2], far_recv.at[i], {"head": head_at(a, 0)}).start()

    for i, (dx, dy) in enumerate(chip_steps):
        for j, ref in ((0, kw), (1, vw)):
            there = ref.at[group_at(nx - dx, dy, 0)]
            remote(there, there, kv_send, kv_recv.at[j, i], {"group": sibling}).wait_recv()
            remote(there, there, kv_pass_send, kv_pass_recv, {"group": sibling}).start()

    nfar = len(far_steps)
    npass = nfar * len(near_steps) - 1
    for i, a in reversed(list(enumerate(far_steps))):
        there = norm_pick.at[head_at(nz - a, 0)]
        remote(there, there, phase_send.at[2], far_recv.at[i], {"head": head_at(a, 0)}).wait_recv()
        for b, dy in near_steps:
            if (a + b) % nz or dy:
                remote(there, there, phase_send.at[6], phase_recv.at[2], {"head": head_at(b, dy)}).start()
    for i in (0, 1, 3, 4, 9, 11):
        locals_[i].wait()
    total(kw.at[pl.ds(0, 2 * nchip)], kv_pass_send, kv_pass_recv).wait_recv()
    total(norm_pick.at[pl.ds(0, npass)], phase_send.at[6], phase_recv.at[2]).wait_recv()
    for s in range(mem):
        rows = norm_pick[:, s * blk : (s + 1) * blk, :].astype(F32).reshape(seq * chunks, LANES)
        flat[pl.ds(s * seq * chunks, seq * chunks), :] = rows
    rows = mem * seq
    picked = jnp.concatenate([from_flat(flat, 0, rows, c).astype(BF16) for c in range(chunks)], axis=1)

    key_full = kw[...].reshape(dim, width)
    value_full = vw[...].reshape(dim, width)
    keys = mm(picked, key_full, 1, 0).astype(BF16)
    values = mm(picked, value_full, 1, 0).astype(BF16)
    cbias = cross_bias[...]
    qrows = query.shape[0]
    dks, dvs = [], []
    for n in range(nheads):
        cols = slice(n * DK, (n + 1) * DK)
        kept = keep[0, n].astype(F32)
        q_n, g_n = query[:, cols], grad[:, cols]
        k_n, v_n = keys[:, cols], values[:, cols]
        cross = (mm(k_n, q_n, 1, 1) * scale).reshape(mem, seq, qrows) + cbias[None]
        cross = cross.reshape(rows, qrows)
        e = jnp.exp(cross - jnp.max(cross, axis=0, keepdims=True))
        prob = e * (1.0 / jnp.sum(e, axis=0, keepdims=True))
        prob_low = prob.astype(BF16)
        context[:, cols] = (mm(prob_low, v_n, 0, 0) * kept).astype(BF16)
        dprob = mm(v_n, g_n, 1, 1)
        delta = jnp.sum(prob * dprob, axis=0, keepdims=True)
        dscore = (prob * (dprob - delta) * (scale * kept)).astype(BF16)
        dks.append(mm(dscore, q_n, 1, 0).astype(BF16))
        dvs.append((mm(prob_low, g_n, 1, 0) * kept).astype(BF16))
    dks = jnp.concatenate(dks, axis=1)
    dvs = jnp.concatenate(dvs, axis=1)
    dnorm = mm(dks, key_full, 1, 1) + mm(dvs, value_full, 1, 1)

    to_flat(dnorm, flat, 0)
    for s in range(mem):
        block = flat[pl.ds(s * seq * chunks, seq * chunks), :].reshape(nhead, blk, LANES)
        dn_send[:, s * blk : (s + 1) * blk, :] = block.astype(BF16)

    for i, a in enumerate(far_steps):
        for j, (b, dy) in enumerate(near_steps):
            there = dn_send.at[head_at(a + b, dy)]
            remote(there, dn_near.at[i, j], phase_send.at[3], near_recv.at[i], {"head": head_at(b, dy)}).start()
    for i, a in enumerate(far_steps):
        total(dn_near.at[i], phase_send.at[3], near_recv.at[i]).wait_recv()
        near = dn_send[head_at(a, 0)].astype(F32) + jnp.sum(dn_near[i].astype(F32), axis=0)
        dn_sum[i] = near.astype(BF16)
        remote(dn_sum.at[i], dn_far.at[i], phase_send.at[7], phase_recv.at[3], {"head": head_at(a, 0)}).start()
    total(dn_far, phase_send.at[7], phase_recv.at[3]).wait_recv()
    dn_all[g] = jnp.sum(dn_far[...].astype(F32), axis=0).astype(BF16)

    there = dn_all.at[g]
    for step in group_steps:
        remote(there, there, phase_send.at[4], phase_recv.at[4], {"group": group_at(*step)}).start()
    total(dn_all.at[pl.ds(0, ngroup - 1)], phase_send.at[4], phase_recv.at[4]).wait_recv()
    acc = jnp.zeros((blk, LANES), F32)
    for d in range(ngroup):
        for s in range(mem):
            block = dn_all[d, s * blk : (s + 1) * blk, :].astype(F32)
            acc = acc + block * (sources[s, d] == g).astype(F32)
    scaled = acc * gains
    mg_all[h] = (inv * (scaled - normed * row_mean(scaled * normed))).astype(BF16)

    def send_mg(k):
        there = mg_all.at[h]
        remote(there, there, phase_send.at[5], phase_recv.at[5], {"head": head_peer(k)}).start()

    each(nhead, send_mg)
    total(mg_all.at[pl.ds(0, nhead - 1)], phase_send.at[5], phase_recv.at[5]).wait_recv()
    flat[pl.ds(0, seq * chunks), :] = mg_all[...].astype(F32).reshape(seq * chunks, LANES)
    for c in range(chunks):
        memory_grad[:, c * LANES : (c + 1) * LANES] = from_flat(flat, 0, seq, c).astype(BF16)

    total(wo.at[pl.ds(0, nchip - 1)], wo_send, wo_recv.at[0]).wait_send()
    total(wo.at[pl.ds(0, nchip)], wo_pass_send, wo_pass_recv).wait_send()
    total(kw.at[pl.ds(0, 2 * nchip - 2)], kv_send, kv_recv.at[0, 0]).wait_send()
    total(kw.at[pl.ds(0, 2 * nchip)], kv_pass_send, kv_pass_recv).wait_send()
    sent = (
        out_recv,
        norm_all.at[pl.ds(0, ngroup - 1)],
        norm_pick.at[pl.ds(0, nfar)],
        dn_near,
        dn_all.at[pl.ds(0, ngroup - 1)],
        mg_all.at[pl.ds(0, nhead - 1)],
        norm_pick.at[pl.ds(0, npass)],
        dn_far,
    )
    for i, ref in enumerate(sent):
        total(ref, phase_send.at[i], phase_recv.at[0]).wait_send()


def shards(
    ngroup,
    nhead,
    enc_resid,
    enc_qkv,
    enc_bias,
    out_weight,
    final_gain,
    key_weight,
    value_weight,
    dec_query,
    cross_bias,
    out_grad,
    sources,
    head_keep,
):
    seq, dim = enc_resid.shape
    qrows, width = dec_query.shape
    mem = sources.shape[1]
    chunks = dim // LANES
    blk = seq // nhead * chunks
    nchip = ngroup // 2
    nfar = nhead // 8
    vmem = pl.BlockSpec(memory_space=pltpu.VMEM)
    hbm = pl.BlockSpec(memory_space=pltpu.HBM)
    dma = pltpu.SemaphoreType.DMA
    operands = (
        sources.T,
        head_keep,
        enc_resid,
        enc_qkv,
        enc_bias,
        final_gain.reshape(chunks, LANES),
        cross_bias.T,
        out_weight,
        key_weight,
        value_weight,
        dec_query,
        out_grad,
    )
    return tuple(
        pl.pallas_call(
            functools.partial(kernel, ngroup, nhead, mem),
            out_shape=(
                pltpu.VMEM((qrows, width), BF16),
                pltpu.VMEM((seq, dim), BF16),
            ),
            in_specs=[hbm] * 12,
            out_specs=(vmem, vmem),
            scratch_shapes=[
                pltpu.SMEM(sources.shape[::-1], jnp.int32),
                pltpu.SMEM(head_keep.shape, jnp.int32),
                pltpu.VMEM(enc_resid.shape, BF16),
                pltpu.VMEM(enc_qkv.shape, BF16),
                pltpu.VMEM(enc_bias.shape, F32),
                pltpu.VMEM((chunks, LANES), F32),
                pltpu.VMEM(cross_bias.shape[::-1], F32),
                pltpu.VMEM((ngroup,) + out_weight.shape, BF16),
                pltpu.VMEM((ngroup,) + key_weight.shape, BF16),
                pltpu.VMEM((ngroup,) + value_weight.shape, BF16),
                pltpu.VMEM((qrows, width), BF16),
                pltpu.VMEM((qrows, width), BF16),
                pltpu.VMEM((mem * seq * chunks, LANES), F32),
                pltpu.VMEM((seq * chunks, LANES), F32),
                pltpu.VMEM((nhead, blk, LANES), BF16),
                pltpu.VMEM((nhead - 1, blk, LANES), BF16),
                pltpu.VMEM((ngroup, blk, LANES), BF16),
                pltpu.VMEM((nhead, mem * blk, LANES), BF16),
                pltpu.VMEM((nhead, mem * blk, LANES), BF16),
                pltpu.VMEM((nfar, 7, mem * blk, LANES), BF16),
                pltpu.VMEM((nfar, mem * blk, LANES), BF16),
                pltpu.VMEM((nfar, mem * blk, LANES), BF16),
                pltpu.VMEM((ngroup, mem * blk, LANES), BF16),
                pltpu.VMEM((nhead, blk, LANES), BF16),
                dma((12,)),
                dma,
                dma((nchip,)),
                dma,
                dma,
                dma,
                dma((2, nchip)),
                dma,
                dma,
                dma((nfar,)),
                dma((nfar,)),
                dma((8,)),
                dma((6,)),
            ],
            compiler_params=pltpu.CompilerParams(
                collective_id=0, has_side_effects=True, vmem_limit_bytes=40 * 1024 * 1024
            ),
        )(
            *(pltpu.with_memory_space_constraint(x, pltpu.HBM) for x in operands),
        )
    )


def solution(mesh):
    in_specs = (
        P("group", None),
        P(None, "group", "head"),
        P(),
        P(("head", "group"), None),
        P(),
        P("group", "head"),
        P("group", "head"),
        P("group", "head"),
        P(),
        P("group", "head"),
        P(),
        P("group", "head"),
    )
    out_specs = (P("group", "head"), P("group", None))
    step = functools.partial(shards, mesh.shape["group"], mesh.shape["head"])
    return jax.shard_map(step, mesh=mesh, in_specs=in_specs, out_specs=out_specs, check_vma=False)
```

```python
import functools
import math

import jax
import jax.numpy as jnp
from jax import lax
from jax.experimental import pallas as pl
from jax.experimental.pallas import tpu as pltpu
from jax.sharding import PartitionSpec as P

MESH = pl.DeviceIdType.MESH
BF16 = jnp.bfloat16
F32 = jnp.float32
DK = 128
LANES = 128
EPS = 1e-06


def mm(a, b, ca, cb):
    return lax.dot_general(a, b, (((ca,), (cb,)), ((), ())), preferred_element_type=F32)


def kernel(
    ngroup,
    nhead,
    mem,
    sources_hbm,
    keep_hbm,
    resid_hbm,
    qkv_hbm,
    enc_bias_hbm,
    gain_hbm,
    cross_bias_hbm,
    out_w,
    key_w,
    value_w,
    query_hbm,
    grad_hbm,
    context,
    memory_grad,
    sources,
    keep,
    resid,
    qkv,
    enc_bias,
    gain,
    cross_bias,
    wo,
    kw,
    vw,
    query,
    grad,
    flat,
    resid_flat,
    out_send,
    out_recv,
    norm_all,
    norm_pick,
    dn_send,
    dn_near,
    dn_sum,
    dn_far,
    dn_all,
    mg_all,
    local_sem,
    wo_send,
    wo_recv,
    wo_pass_send,
    wo_pass_recv,
    kv_send,
    kv_recv,
    kv_pass_send,
    kv_pass_recv,
    far_recv,
    near_recv,
    phase_send,
    phase_recv,
    ready,
):
    seq, dim = resid.shape
    width = query.shape[1]
    nheads = width // DK
    chunks = dim // LANES
    own_rows = seq // nhead
    blk = own_rows * chunks
    scale = 1.0 / math.sqrt(DK)
    g = lax.axis_index("group")
    h = lax.axis_index("head")
    core = lax.rem(g, 2)
    chip = lax.div(g, 2)
    sibling = g + 1 - 2 * core
    nchip = ngroup // 2

    nz, nx = nhead // 2, ngroup // 4
    z, y = lax.div(h, 2), lax.rem(h, 2)
    gx, gy = lax.div(g, 4), lax.rem(lax.div(g, 2), 2)

    def each(n, body):
        lax.fori_loop(1, n, lambda k, c: (body(k), c)[1], 0)

    def head_at(dz, dy):
        return lax.rem(z + dz + nz, nz) * 2 + lax.rem(y + dy, 2)

    def group_at(dx, dy, dc):
        return lax.rem(gx + dx, nx) * 4 + lax.rem(gy + dy, 2) * 2 + lax.rem(core + dc, 2)

    def head_peer(k):
        j = lax.div(k - 1, 2)
        away = nz // 2 - lax.div(j + 1, 2)
        return head_at(away * (2 * lax.rem(j, 2) - 1), lax.rem(k, 2))

    def spread(dx, dy, dc):
        return -(min(dx, nx - dx) * 4 + dy * 4 + dc)

    steps = [(dx, dy, dc) for dx in range(nx) for dy in range(2) for dc in range(2)][1:]
    group_steps = sorted(steps, key=lambda t: spread(*t))
    chip_steps = [(dx, dy) for dx, dy, dc in group_steps if dc == 0]
    far_steps = sorted(range(2, nz, 4), key=lambda a: -min(a, nz - a))
    near_steps = [(2, 1), (1, 1), (nz - 1, 1), (0, 1), (2, 0), (1, 0), (nz - 1, 0)]

    def remote(src, dst, send, recv, where):
        return pltpu.make_async_remote_copy(
            src_ref=src,
            dst_ref=dst,
            send_sem=send,
            recv_sem=recv,
            device_id=where,
            device_id_type=MESH,
        )

    def total(ref, send, recv):
        return remote(ref, ref, send, recv, {"group": sibling})

    barrier = pltpu.get_barrier_semaphore()
    even, odd = g - core, g - core + 1

    def hello(**where):
        pl.semaphore_signal(barrier, inc=1, device_id=where, device_id_type=MESH)

    def tell_sibling():
        pl.semaphore_signal(ready, inc=1, device_id={"group": sibling}, device_id_type=MESH)

    each(nchip, lambda k: hello(group=lax.rem(chip + k, nchip) * 2))
    pl.when(core == 1)(lambda: hello(group=even))
    each(nhead, lambda k: hello(group=odd, head=head_peer(k)))
    locals_ = [
        pltpu.make_async_copy(query_hbm, query, local_sem.at[0]),
        pltpu.make_async_copy(grad_hbm, grad, local_sem.at[1]),
        pltpu.make_async_copy(out_w, wo.at[g], local_sem.at[2]),
        pltpu.make_async_copy(key_w, kw.at[g], local_sem.at[3]),
        pltpu.make_async_copy(value_w, vw.at[g], local_sem.at[4]),
        pltpu.make_async_copy(qkv_hbm, qkv, local_sem.at[5]),
        pltpu.make_async_copy(enc_bias_hbm, enc_bias, local_sem.at[6]),
        pltpu.make_async_copy(resid_hbm, resid, local_sem.at[7]),
        pltpu.make_async_copy(gain_hbm, gain, local_sem.at[8]),
        pltpu.make_async_copy(cross_bias_hbm, cross_bias, local_sem.at[9]),
        pltpu.make_async_copy(sources_hbm, sources, local_sem.at[10]),
        pltpu.make_async_copy(keep_hbm, keep, local_sem.at[11]),
    ]
    for copy in locals_:
        copy.start()

    @pl.when(core == 0)
    def _():
        pl.semaphore_wait(barrier, ngroup - 1)
        tell_sibling()

    @pl.when(core == 1)
    def _():
        pl.semaphore_wait(ready, 1)

    for i, (dx, dy) in enumerate(chip_steps):
        remote(out_w, wo.at[g], wo_send, wo_recv.at[i], {"group": group_at(dx, dy, 0)}).start()
    remote(out_w, wo.at[g], wo_pass_send, wo_pass_recv, {"group": sibling}).start()

    locals_[5].wait()
    locals_[6].wait()
    bias = enc_bias[...]
    ctx = []
    for n in range(nheads):
        cols = slice(n * DK, (n + 1) * DK)
        scores = mm(qkv[0, :, cols], qkv[1, :, cols], 1, 1) * scale + bias
        e = jnp.exp(scores - jnp.max(scores, axis=1, keepdims=True))
        p = (e * (1.0 / jnp.sum(e, axis=1, keepdims=True))).astype(BF16)
        ctx.append(mm(p, qkv[2, :, cols], 1, 0).astype(BF16))
    ctx = jnp.concatenate(ctx, axis=1)

    def to_flat(x, ref, base):
        rows = x.shape[0]
        for c in range(chunks):
            ref[pl.ds(base * chunks + c, rows, stride=chunks), :] = x[:, c * LANES : (c + 1) * LANES]

    def from_flat(ref, base, rows, c):
        return ref[pl.ds(base * chunks + c, rows, stride=chunks), :]

    locals_[7].wait()
    to_flat(resid[...].astype(F32), resid_flat, 0)

    for i, (dx, dy) in enumerate(chip_steps):
        there = wo.at[group_at(nx - dx, dy, 0)]
        remote(there, there, wo_send, wo_recv.at[i], {"group": sibling}).wait_recv()
        remote(there, there, wo_pass_send, wo_pass_recv, {"group": sibling}).start()

    @pl.when(core == 1)
    def _():
        pl.semaphore_wait(barrier, 2 * (nhead - 1))
        tell_sibling()

    locals_[2].wait()
    total(wo.at[pl.ds(0, nchip)], wo_pass_send, wo_pass_recv).wait_recv()
    part = mm(ctx, wo[...].reshape(width, dim), 1, 0)

    to_flat(part, flat, 0)
    out_send[...] = flat[pl.ds(0, seq * chunks), :].reshape(nhead, blk, LANES).astype(BF16)

    def send_out(k):
        there = head_peer(k)
        remote(out_send.at[there], out_recv.at[k - 1], phase_send.at[0], phase_recv.at[0], {"head": there}).start()

    @pl.when(core == 0)
    def _():
        pl.semaphore_wait(ready, 1)

    each(nhead, send_out)

    for i, (dx, dy) in enumerate(chip_steps):
        where = {"group": group_at(dx, dy, 0)}
        remote(key_w, kw.at[g], kv_send, kv_recv.at[0, i], where).start()
        remote(value_w, vw.at[g], kv_send, kv_recv.at[1, i], where).start()
    remote(key_w, kw.at[g], kv_pass_send, kv_pass_recv, {"group": sibling}).start()
    remote(value_w, vw.at[g], kv_pass_send, kv_pass_recv, {"group": sibling}).start()

    mine = pl.ds(pl.multiple_of(h * blk, blk), blk)
    memory = flat[mine, :] + resid_flat[mine, :]
    total(out_recv, phase_send.at[0], phase_recv.at[0]).wait_recv()
    memory = memory + jnp.sum(out_recv[...].astype(F32), axis=0)

    def row_mean(x):
        x3 = x.reshape(own_rows, chunks, LANES)
        m = jnp.sum(jnp.sum(x3, axis=1, keepdims=True), axis=2, keepdims=True) * (1.0 / dim)
        return jnp.broadcast_to(m, x3.shape).reshape(blk, LANES)

    locals_[8].wait()
    gains = jnp.broadcast_to(gain[...][None], (own_rows, chunks, LANES)).reshape(blk, LANES)
    inv = lax.rsqrt(row_mean(memory * memory) + EPS)
    normed = memory * inv
    norm_all[g] = (normed * gains).astype(BF16)

    there = norm_all.at[g]
    for step in group_steps:
        remote(there, there, phase_send.at[1], phase_recv.at[1], {"group": group_at(*step)}).start()
    total(norm_all.at[pl.ds(0, ngroup - 1)], phase_send.at[1], phase_recv.at[1]).wait_recv()

    locals_[10].wait()
    for s in range(mem):
        norm_pick[h, s * blk : (s + 1) * blk, :] = norm_all[sources[s, g]]

    there = norm_pick.at[h]
    for i, a in enumerate(far_steps):
        remote(there, there, phase_send.at[2], far_recv.at[i], {"head": head_at(a, 0)}).start()

    for i, (dx, dy) in enumerate(chip_steps):
        for j, ref in ((0, kw), (1, vw)):
            there = ref.at[group_at(nx - dx, dy, 0)]
            remote(there, there, kv_send, kv_recv.at[j, i], {"group": sibling}).wait_recv()
            remote(there, there, kv_pass_send, kv_pass_recv, {"group": sibling}).start()

    nfar = len(far_steps)
    npass = nfar * len(near_steps) - 1
    for i, a in reversed(list(enumerate(far_steps))):
        there = norm_pick.at[head_at(nz - a, 0)]
        remote(there, there, phase_send.at[2], far_recv.at[i], {"head": head_at(a, 0)}).wait_recv()
        for b, dy in near_steps:
            if (a + b) % nz or dy:
                remote(there, there, phase_send.at[6], phase_recv.at[2], {"head": head_at(b, dy)}).start()
    for i in (0, 1, 3, 4, 9, 11):
        locals_[i].wait()
    total(kw.at[pl.ds(0, 2 * nchip)], kv_pass_send, kv_pass_recv).wait_recv()
    total(norm_pick.at[pl.ds(0, npass)], phase_send.at[6], phase_recv.at[2]).wait_recv()
    for s in range(mem):
        rows = norm_pick[:, s * blk : (s + 1) * blk, :].astype(F32).reshape(seq * chunks, LANES)
        flat[pl.ds(s * seq * chunks, seq * chunks), :] = rows
    rows = mem * seq
    picked = jnp.concatenate([from_flat(flat, 0, rows, c).astype(BF16) for c in range(chunks)], axis=1)

    key_full = kw[...].reshape(dim, width)
    value_full = vw[...].reshape(dim, width)
    keys = mm(picked, key_full, 1, 0).astype(BF16)
    values = mm(picked, value_full, 1, 0).astype(BF16)
    cbias = cross_bias[...]
    qrows = query.shape[0]
    dks, dvs = [], []
    for n in range(nheads):
        cols = slice(n * DK, (n + 1) * DK)
        kept = keep[0, n].astype(F32)
        q_n, g_n = query[:, cols], grad[:, cols]
        k_n, v_n = keys[:, cols], values[:, cols]
        cross = (mm(k_n, q_n, 1, 1) * scale).reshape(mem, seq, qrows) + cbias[None]
        cross = cross.reshape(rows, qrows)
        e = jnp.exp(cross - jnp.max(cross, axis=0, keepdims=True))
        prob = e * (1.0 / jnp.sum(e, axis=0, keepdims=True))
        prob_low = prob.astype(BF16)
        context[:, cols] = (mm(prob_low, v_n, 0, 0) * kept).astype(BF16)
        dprob = mm(v_n, g_n, 1, 1)
        delta = jnp.sum(prob * dprob, axis=0, keepdims=True)
        dscore = (prob * (dprob - delta) * (scale * kept)).astype(BF16)
        dks.append(mm(dscore, q_n, 1, 0).astype(BF16))
        dvs.append((mm(prob_low, g_n, 1, 0) * kept).astype(BF16))
    dks = jnp.concatenate(dks, axis=1)
    dvs = jnp.concatenate(dvs, axis=1)
    dnorm = mm(dks, key_full, 1, 1) + mm(dvs, value_full, 1, 1)

    to_flat(dnorm, flat, 0)
    for s in range(mem):
        block = flat[pl.ds(s * seq * chunks, seq * chunks), :].reshape(nhead, blk, LANES)
        dn_send[:, s * blk : (s + 1) * blk, :] = block.astype(BF16)

    for i, a in enumerate(far_steps):
        for j, (b, dy) in enumerate(near_steps):
            there = dn_send.at[head_at(a + b, dy)]
            remote(there, dn_near.at[i, j], phase_send.at[3], near_recv.at[i], {"head": head_at(b, dy)}).start()
    for i, a in enumerate(far_steps):
        total(dn_near.at[i], phase_send.at[3], near_recv.at[i]).wait_recv()
        near = dn_send[head_at(a, 0)].astype(F32) + jnp.sum(dn_near[i].astype(F32), axis=0)
        dn_sum[i] = near.astype(BF16)
        remote(dn_sum.at[i], dn_far.at[i], phase_send.at[7], phase_recv.at[3], {"head": head_at(a, 0)}).start()
    total(dn_far, phase_send.at[7], phase_recv.at[3]).wait_recv()
    dn_all[g] = jnp.sum(dn_far[...].astype(F32), axis=0).astype(BF16)

    there = dn_all.at[g]
    for step in group_steps:
        remote(there, there, phase_send.at[4], phase_recv.at[4], {"group": group_at(*step)}).start()
    total(dn_all.at[pl.ds(0, ngroup - 1)], phase_send.at[4], phase_recv.at[4]).wait_recv()
    acc = jnp.zeros((blk, LANES), F32)
    for d in range(ngroup):
        for s in range(mem):
            block = dn_all[d, s * blk : (s + 1) * blk, :].astype(F32)
            acc = acc + block * (sources[s, d] == g).astype(F32)
    scaled = acc * gains
    mg_all[h] = (inv * (scaled - normed * row_mean(scaled * normed))).astype(BF16)

    def send_mg(k):
        there = mg_all.at[h]
        remote(there, there, phase_send.at[5], phase_recv.at[5], {"head": head_peer(k)}).start()

    each(nhead, send_mg)
    total(mg_all.at[pl.ds(0, nhead - 1)], phase_send.at[5], phase_recv.at[5]).wait_recv()
    flat[pl.ds(0, seq * chunks), :] = mg_all[...].astype(F32).reshape(seq * chunks, LANES)
    for c in range(chunks):
        memory_grad[:, c * LANES : (c + 1) * LANES] = from_flat(flat, 0, seq, c).astype(BF16)

    total(wo.at[pl.ds(0, nchip - 1)], wo_send, wo_recv.at[0]).wait_send()
    total(wo.at[pl.ds(0, nchip)], wo_pass_send, wo_pass_recv).wait_send()
    total(kw.at[pl.ds(0, 2 * nchip - 2)], kv_send, kv_recv.at[0, 0]).wait_send()
    total(kw.at[pl.ds(0, 2 * nchip)], kv_pass_send, kv_pass_recv).wait_send()
    sent = (
        out_recv,
        norm_all.at[pl.ds(0, ngroup - 1)],
        norm_pick.at[pl.ds(0, nfar)],
        dn_near,
        dn_all.at[pl.ds(0, ngroup - 1)],
        mg_all.at[pl.ds(0, nhead - 1)],
        norm_pick.at[pl.ds(0, npass)],
        dn_far,
    )
    for i, ref in enumerate(sent):
        total(ref, phase_send.at[i], phase_recv.at[0]).wait_send()


def shards(
    ngroup,
    nhead,
    enc_resid,
    enc_qkv,
    enc_bias,
    out_weight,
    final_gain,
    key_weight,
    value_weight,
    dec_query,
    cross_bias,
    out_grad,
    sources,
    head_keep,
):
    seq, dim = enc_resid.shape
    qrows, width = dec_query.shape
    mem = sources.shape[1]
    chunks = dim // LANES
    blk = seq // nhead * chunks
    nchip = ngroup // 2
    nfar = nhead // 8
    vmem = pl.BlockSpec(memory_space=pltpu.VMEM)
    hbm = pl.BlockSpec(memory_space=pltpu.HBM)
    dma = pltpu.SemaphoreType.DMA
    operands = (
        sources.T,
        head_keep,
        enc_resid,
        enc_qkv,
        enc_bias,
        final_gain.reshape(chunks, LANES),
        cross_bias.T,
        out_weight,
        key_weight,
        value_weight,
        dec_query,
        out_grad,
    )
    return tuple(
        pl.pallas_call(
            functools.partial(kernel, ngroup, nhead, mem),
            out_shape=(
                pltpu.VMEM((qrows, width), BF16),
                pltpu.VMEM((seq, dim), BF16),
            ),
            in_specs=[hbm] * 12,
            out_specs=(vmem, vmem),
            scratch_shapes=[
                pltpu.SMEM(sources.shape[::-1], jnp.int32),
                pltpu.SMEM(head_keep.shape, jnp.int32),
                pltpu.VMEM(enc_resid.shape, BF16),
                pltpu.VMEM(enc_qkv.shape, BF16),
                pltpu.VMEM(enc_bias.shape, F32),
                pltpu.VMEM((chunks, LANES), F32),
                pltpu.VMEM(cross_bias.shape[::-1], F32),
                pltpu.VMEM((ngroup,) + out_weight.shape, BF16),
                pltpu.VMEM((ngroup,) + key_weight.shape, BF16),
                pltpu.VMEM((ngroup,) + value_weight.shape, BF16),
                pltpu.VMEM((qrows, width), BF16),
                pltpu.VMEM((qrows, width), BF16),
                pltpu.VMEM((mem * seq * chunks, LANES), F32),
                pltpu.VMEM((seq * chunks, LANES), F32),
                pltpu.VMEM((nhead, blk, LANES), BF16),
                pltpu.VMEM((nhead - 1, blk, LANES), BF16),
                pltpu.VMEM((ngroup, blk, LANES), BF16),
                pltpu.VMEM((nhead, mem * blk, LANES), BF16),
                pltpu.VMEM((nhead, mem * blk, LANES), BF16),
                pltpu.VMEM((nfar, 7, mem * blk, LANES), BF16),
                pltpu.VMEM((nfar, mem * blk, LANES), BF16),
                pltpu.VMEM((nfar, mem * blk, LANES), BF16),
                pltpu.VMEM((ngroup, mem * blk, LANES), BF16),
                pltpu.VMEM((nhead, blk, LANES), BF16),
                dma((12,)),
                dma,
                dma((nchip,)),
                dma,
                dma,
                dma,
                dma((2, nchip)),
                dma,
                dma,
                dma((nfar,)),
                dma((nfar,)),
                dma((8,)),
                dma((6,)),
                pltpu.SemaphoreType.REGULAR,
            ],
            compiler_params=pltpu.CompilerParams(
                collective_id=0, has_side_effects=True, vmem_limit_bytes=40 * 1024 * 1024
            ),
        )(
            *(pltpu.with_memory_space_constraint(x, pltpu.HBM) for x in operands),
        )
    )


def solution(mesh):
    in_specs = (
        P("group", None),
        P(None, "group", "head"),
        P(),
        P(("head", "group"), None),
        P(),
        P("group", "head"),
        P("group", "head"),
        P("group", "head"),
        P(),
        P("group", "head"),
        P(),
        P("group", "head"),
    )
    out_specs = (P("group", "head"), P("group", None))
    step = functools.partial(shards, mesh.shape["group"], mesh.shape["head"])
    return jax.shard_map(step, mesh=mesh, in_specs=in_specs, out_specs=out_specs, check_vma=False)
```

```python
import functools
import math

import jax
import jax.numpy as jnp
from jax import lax
from jax.experimental import pallas as pl
from jax.experimental.pallas import tpu as pltpu
from jax.sharding import PartitionSpec as P

MESH = pl.DeviceIdType.MESH
BF16 = jnp.bfloat16
F32 = jnp.float32
DK = 128
LANES = 128
EPS = 1e-06


def mm(a, b, ca, cb):
    return lax.dot_general(a, b, (((ca,), (cb,)), ((), ())), preferred_element_type=F32)


def kernel(
    ngroup,
    nhead,
    mem,
    sources_hbm,
    keep_hbm,
    resid_hbm,
    qkv_hbm,
    enc_bias_hbm,
    gain_hbm,
    cross_bias_hbm,
    out_w,
    key_w,
    value_w,
    query_hbm,
    grad_hbm,
    context,
    memory_grad,
    sources,
    keep,
    resid,
    qkv,
    enc_bias,
    gain,
    cross_bias,
    wo,
    kw,
    vw,
    query,
    grad,
    flat,
    resid_flat,
    out_send,
    out_recv,
    norm_all,
    norm_pick,
    dn_send,
    dn_near,
    dn_sum,
    dn_far,
    probs,
    pick,
    dn_out,
    dn_in,
    mg_all,
    local_sem,
    wo_send,
    wo_recv,
    wo_pass_send,
    wo_pass_recv,
    kv_send,
    kv_recv,
    kv_pass_send,
    kv_pass_recv,
    far_recv,
    near_recv,
    phase_send,
    phase_recv,
    ready,
):
    seq, dim = resid.shape
    width = query.shape[1]
    nheads = width // DK
    chunks = dim // LANES
    own_rows = seq // nhead
    blk = own_rows * chunks
    scale = 1.0 / math.sqrt(DK)
    g = lax.axis_index("group")
    h = lax.axis_index("head")
    core = lax.rem(g, 2)
    chip = lax.div(g, 2)
    sibling = g + 1 - 2 * core
    nchip = ngroup // 2

    nz, nx = nhead // 2, ngroup // 4
    z, y = lax.div(h, 2), lax.rem(h, 2)
    gx, gy = lax.div(g, 4), lax.rem(lax.div(g, 2), 2)

    def each(n, body):
        lax.fori_loop(1, n, lambda k, c: (body(k), c)[1], 0)

    def head_at(dz, dy):
        return lax.rem(z + dz + nz, nz) * 2 + lax.rem(y + dy, 2)

    def group_at(dx, dy, dc):
        return lax.rem(gx + dx, nx) * 4 + lax.rem(gy + dy, 2) * 2 + lax.rem(core + dc, 2)

    head_steps = sorted(
        [(dz, dy) for dz in range(nz) for dy in range(2)][1:], key=lambda t: -(min(t[0], nz - t[0]) * 2 + t[1])
    )

    def head_peer(k):
        j = lax.div(k - 1, 2)
        away = nz // 2 - lax.div(j + 1, 2)
        return head_at(away * (2 * lax.rem(j, 2) - 1), lax.rem(k, 2))

    def spread(dx, dy, dc):
        return -(min(dx, nx - dx) * 4 + dy * 4 + dc)

    steps = [(dx, dy, dc) for dx in range(nx) for dy in range(2) for dc in range(2)][1:]
    group_steps = sorted(steps, key=lambda t: spread(*t))
    chip_steps = [(dx, dy) for dx, dy, dc in group_steps if dc == 0]
    far_steps = sorted(range(2, nz, 4), key=lambda a: -min(a, nz - a))
    near_steps = [(2, 1), (1, 1), (nz - 1, 1), (0, 1), (2, 0), (1, 0), (nz - 1, 0)]

    def remote(src, dst, send, recv, where):
        return pltpu.make_async_remote_copy(
            src_ref=src,
            dst_ref=dst,
            send_sem=send,
            recv_sem=recv,
            device_id=where,
            device_id_type=MESH,
        )

    def total(ref, send, recv):
        return remote(ref, ref, send, recv, {"group": sibling})

    barrier = pltpu.get_barrier_semaphore()
    even, odd = g - core, g - core + 1

    def hello(**where):
        pl.semaphore_signal(barrier, inc=1, device_id=where, device_id_type=MESH)

    def tell_sibling():
        pl.semaphore_signal(ready, inc=1, device_id={"group": sibling}, device_id_type=MESH)

    each(nchip, lambda k: hello(group=lax.rem(chip + k, nchip) * 2))
    pl.when(core == 1)(lambda: hello(group=even))
    each(nhead, lambda k: hello(group=odd, head=head_peer(k)))
    locals_ = [
        pltpu.make_async_copy(query_hbm, query, local_sem.at[0]),
        pltpu.make_async_copy(grad_hbm, grad, local_sem.at[1]),
        pltpu.make_async_copy(out_w, wo.at[g], local_sem.at[2]),
        pltpu.make_async_copy(key_w, kw.at[g], local_sem.at[3]),
        pltpu.make_async_copy(value_w, vw.at[g], local_sem.at[4]),
        pltpu.make_async_copy(qkv_hbm, qkv, local_sem.at[5]),
        pltpu.make_async_copy(enc_bias_hbm, enc_bias, local_sem.at[6]),
        pltpu.make_async_copy(resid_hbm, resid, local_sem.at[7]),
        pltpu.make_async_copy(gain_hbm, gain, local_sem.at[8]),
        pltpu.make_async_copy(cross_bias_hbm, cross_bias, local_sem.at[9]),
        pltpu.make_async_copy(sources_hbm, sources, local_sem.at[10]),
        pltpu.make_async_copy(keep_hbm, keep, local_sem.at[11]),
    ]
    for copy in locals_:
        copy.start()

    @pl.when(core == 0)
    def _():
        pl.semaphore_wait(barrier, ngroup - 1)
        tell_sibling()

    @pl.when(core == 1)
    def _():
        pl.semaphore_wait(ready, 1)

    for i, (dx, dy) in enumerate(chip_steps):
        remote(out_w, wo.at[g], wo_send, wo_recv.at[i], {"group": group_at(dx, dy, 0)}).start()
    remote(out_w, wo.at[g], wo_pass_send, wo_pass_recv, {"group": sibling}).start()

    locals_[5].wait()
    locals_[6].wait()
    bias = enc_bias[...]
    ctx = []
    for n in range(nheads):
        cols = slice(n * DK, (n + 1) * DK)
        scores = mm(qkv[0, :, cols], qkv[1, :, cols], 1, 1) * scale + bias
        e = jnp.exp(scores - jnp.max(scores, axis=1, keepdims=True))
        p = (e * (1.0 / jnp.sum(e, axis=1, keepdims=True))).astype(BF16)
        ctx.append(mm(p, qkv[2, :, cols], 1, 0).astype(BF16))
    ctx = jnp.concatenate(ctx, axis=1)

    def to_flat(x, ref, base):
        rows = x.shape[0]
        for c in range(chunks):
            ref[pl.ds(base * chunks + c, rows, stride=chunks), :] = x[:, c * LANES : (c + 1) * LANES]

    def from_flat(ref, base, rows, c):
        return ref[pl.ds(base * chunks + c, rows, stride=chunks), :]

    locals_[7].wait()
    to_flat(resid[...].astype(F32), resid_flat, 0)

    locals_[10].wait()
    for e in range(ngroup):
        for s in range(mem):
            reads = (sources[s, g] == e).astype(jnp.int32)
            pick[e * mem + s] = jnp.full((blk, LANES), reads, jnp.int32).astype(F32)

    for i, (dx, dy) in enumerate(chip_steps):
        there = wo.at[group_at(nx - dx, dy, 0)]
        remote(there, there, wo_send, wo_recv.at[i], {"group": sibling}).wait_recv()
        remote(there, there, wo_pass_send, wo_pass_recv, {"group": sibling}).start()

    @pl.when(core == 1)
    def _():
        pl.semaphore_wait(barrier, 2 * (nhead - 1))
        tell_sibling()

    locals_[2].wait()
    total(wo.at[pl.ds(0, nchip)], wo_pass_send, wo_pass_recv).wait_recv()
    part = mm(ctx, wo[...].reshape(width, dim), 1, 0)

    to_flat(part, flat, 0)
    out_send[...] = flat[pl.ds(0, seq * chunks), :].reshape(nhead, blk, LANES).astype(BF16)

    @pl.when(core == 0)
    def _():
        pl.semaphore_wait(ready, 1)

    for i, step in enumerate(head_steps):
        there = head_at(*step)
        remote(out_send.at[there], out_recv.at[i], phase_send.at[0], phase_recv.at[0], {"head": there}).start()

    for i, (dx, dy) in enumerate(chip_steps):
        remote(key_w, kw.at[g], kv_send, kv_recv.at[0, i], {"group": group_at(dx, dy, 0)}).start()
    remote(key_w, kw.at[g], kv_pass_send, kv_pass_recv.at[0], {"group": sibling}).start()

    mine = pl.ds(pl.multiple_of(h * blk, blk), blk)
    memory = flat[mine, :] + resid_flat[mine, :]
    total(out_recv, phase_send.at[0], phase_recv.at[0]).wait_recv()
    memory = memory + jnp.sum(out_recv[...].astype(F32), axis=0)

    def row_mean(x):
        x3 = x.reshape(own_rows, chunks, LANES)
        m = jnp.sum(jnp.sum(x3, axis=1, keepdims=True), axis=2, keepdims=True) * (1.0 / dim)
        return jnp.broadcast_to(m, x3.shape).reshape(blk, LANES)

    locals_[8].wait()
    gains = jnp.broadcast_to(gain[...][None], (own_rows, chunks, LANES)).reshape(blk, LANES)
    inv = lax.rsqrt(row_mean(memory * memory) + EPS)
    normed = memory * inv
    norm_all[g] = (normed * gains).astype(BF16)

    there = norm_all.at[g]
    for step in group_steps:
        remote(there, there, phase_send.at[1], phase_recv.at[1], {"group": group_at(*step)}).start()
    total(norm_all.at[pl.ds(0, ngroup - 1)], phase_send.at[1], phase_recv.at[1]).wait_recv()

    for s in range(mem):
        norm_pick[h, s * blk : (s + 1) * blk, :] = norm_all[sources[s, g]]

    there = norm_pick.at[h]
    for i, a in enumerate(far_steps):
        remote(there, there, phase_send.at[2], far_recv.at[i], {"head": head_at(a, 0)}).start()
    for i, (dx, dy) in enumerate(chip_steps):
        remote(value_w, vw.at[g], kv_send, kv_recv.at[1, i], {"group": group_at(dx, dy, 0)}).start()
    remote(value_w, vw.at[g], kv_pass_send, kv_pass_recv.at[1], {"group": sibling}).start()

    def pass_kv(j, ref):
        for i, (dx, dy) in enumerate(chip_steps):
            there = ref.at[group_at(nx - dx, dy, 0)]
            remote(there, there, kv_send, kv_recv.at[j, i], {"group": sibling}).wait_recv()
            remote(there, there, kv_pass_send, kv_pass_recv.at[j], {"group": sibling}).start()

    pass_kv(0, kw)

    nfar = len(far_steps)
    npass = nfar * len(near_steps) - 1
    for i, a in reversed(list(enumerate(far_steps))):
        there = norm_pick.at[head_at(nz - a, 0)]
        remote(there, there, phase_send.at[2], far_recv.at[i], {"head": head_at(a, 0)}).wait_recv()
        for b, dy in near_steps:
            if (a + b) % nz or dy:
                remote(there, there, phase_send.at[6], phase_recv.at[2], {"head": head_at(b, dy)}).start()
    pass_kv(1, vw)
    for i in (0, 3, 9, 11):
        locals_[i].wait()
    total(kw.at[pl.ds(0, nchip)], kv_pass_send, kv_pass_recv.at[0]).wait_recv()
    total(norm_pick.at[pl.ds(0, npass)], phase_send.at[6], phase_recv.at[2]).wait_recv()
    for s in range(mem):
        rows = norm_pick[:, s * blk : (s + 1) * blk, :].astype(F32).reshape(seq * chunks, LANES)
        flat[pl.ds(s * seq * chunks, seq * chunks), :] = rows
    rows = mem * seq
    picked = jnp.concatenate([from_flat(flat, 0, rows, c).astype(BF16) for c in range(chunks)], axis=1)

    key_full = kw[...].reshape(dim, width)
    keys = mm(picked, key_full, 1, 0).astype(BF16)
    cbias = cross_bias[...]
    qrows = query.shape[0]
    for n in range(nheads):
        cols = slice(n * DK, (n + 1) * DK)
        cross = (mm(keys[:, cols], query[:, cols], 1, 1) * scale).reshape(mem, seq, qrows) + cbias[None]
        cross = cross.reshape(rows, qrows)
        e = jnp.exp(cross - jnp.max(cross, axis=0, keepdims=True))
        probs[n] = e * (1.0 / jnp.sum(e, axis=0, keepdims=True))

    locals_[1].wait()
    locals_[4].wait()
    total(vw.at[pl.ds(0, nchip)], kv_pass_send, kv_pass_recv.at[1]).wait_recv()
    value_full = vw[...].reshape(dim, width)
    values = mm(picked, value_full, 1, 0).astype(BF16)
    dks, dvs = [], []
    for n in range(nheads):
        cols = slice(n * DK, (n + 1) * DK)
        kept = keep[0, n].astype(F32)
        q_n, g_n, v_n = query[:, cols], grad[:, cols], values[:, cols]
        prob = probs[n]
        prob_low = prob.astype(BF16)
        context[:, cols] = (mm(prob_low, v_n, 0, 0) * kept).astype(BF16)
        dprob = mm(v_n, g_n, 1, 1)
        delta = jnp.sum(prob * dprob, axis=0, keepdims=True)
        dscore = (prob * (dprob - delta) * (scale * kept)).astype(BF16)
        dks.append(mm(dscore, q_n, 1, 0).astype(BF16))
        dvs.append((mm(prob_low, g_n, 1, 0) * kept).astype(BF16))
    dks = jnp.concatenate(dks, axis=1)
    dvs = jnp.concatenate(dvs, axis=1)
    dnorm = mm(dks, key_full, 1, 1) + mm(dvs, value_full, 1, 1)

    to_flat(dnorm, flat, 0)
    for s in range(mem):
        block = flat[pl.ds(s * seq * chunks, seq * chunks), :].reshape(nhead, blk, LANES)
        dn_send[:, s * blk : (s + 1) * blk, :] = block.astype(BF16)

    for i, a in enumerate(far_steps):
        for j, (b, dy) in enumerate(near_steps):
            there = dn_send.at[head_at(a + b, dy)]
            remote(there, dn_near.at[i, j], phase_send.at[3], near_recv.at[i], {"head": head_at(b, dy)}).start()
    for i, a in enumerate(far_steps):
        total(dn_near.at[i], phase_send.at[3], near_recv.at[i]).wait_recv()
        near = dn_send[head_at(a, 0)].astype(F32) + jnp.sum(dn_near[i].astype(F32), axis=0)
        dn_sum[i] = near.astype(BF16)
        remote(dn_sum.at[i], dn_far.at[i], phase_send.at[7], phase_recv.at[3], {"head": head_at(a, 0)}).start()
    total(dn_far, phase_send.at[7], phase_recv.at[3]).wait_recv()
    dn_sum_all = jnp.sum(dn_far[...].astype(F32), axis=0)

    for e in range(ngroup):
        acc = jnp.zeros((blk, LANES), F32)
        for s in range(mem):
            acc = acc + dn_sum_all[s * blk : (s + 1) * blk] * pick[e * mem + s]
        dn_out[e] = acc.astype(BF16)
    for i, step in enumerate(group_steps):
        there = group_at(*step)
        remote(dn_out.at[there], dn_in.at[i], phase_send.at[4], phase_recv.at[4], {"group": there}).start()
    acc = dn_out[g].astype(F32)
    total(dn_in, phase_send.at[4], phase_recv.at[4]).wait_recv()
    acc = acc + jnp.sum(dn_in[...].astype(F32), axis=0)
    scaled = acc * gains
    mg_all[h] = (inv * (scaled - normed * row_mean(scaled * normed))).astype(BF16)

    there = mg_all.at[h]
    for step in head_steps:
        remote(there, there, phase_send.at[5], phase_recv.at[5], {"head": head_at(*step)}).start()
    total(mg_all.at[pl.ds(0, nhead - 1)], phase_send.at[5], phase_recv.at[5]).wait_recv()
    flat[pl.ds(0, seq * chunks), :] = mg_all[...].astype(F32).reshape(seq * chunks, LANES)
    for c in range(chunks):
        memory_grad[:, c * LANES : (c + 1) * LANES] = from_flat(flat, 0, seq, c).astype(BF16)

    total(wo.at[pl.ds(0, nchip - 1)], wo_send, wo_recv.at[0]).wait_send()
    total(wo.at[pl.ds(0, nchip)], wo_pass_send, wo_pass_recv).wait_send()
    total(kw.at[pl.ds(0, 2 * nchip - 2)], kv_send, kv_recv.at[0, 0]).wait_send()
    total(kw.at[pl.ds(0, 2 * nchip)], kv_pass_send, kv_pass_recv.at[0]).wait_send()
    sent = (
        out_recv,
        norm_all.at[pl.ds(0, ngroup - 1)],
        norm_pick.at[pl.ds(0, nfar)],
        dn_near,
        dn_in,
        mg_all.at[pl.ds(0, nhead - 1)],
        norm_pick.at[pl.ds(0, npass)],
        dn_far,
    )
    for i, ref in enumerate(sent):
        total(ref, phase_send.at[i], phase_recv.at[0]).wait_send()


def store(context, memory_grad, context_hbm, memory_grad_hbm, sem):
    copies = (
        pltpu.make_async_copy(context, context_hbm, sem.at[0]),
        pltpu.make_async_copy(memory_grad, memory_grad_hbm, sem.at[1]),
    )
    for copy in copies:
        copy.start()
    for copy in copies:
        copy.wait()


def shards(
    ngroup,
    nhead,
    enc_resid,
    enc_qkv,
    enc_bias,
    out_weight,
    final_gain,
    key_weight,
    value_weight,
    dec_query,
    cross_bias,
    out_grad,
    sources,
    head_keep,
):
    seq, dim = enc_resid.shape
    qrows, width = dec_query.shape
    mem = sources.shape[1]
    chunks = dim // LANES
    blk = seq // nhead * chunks
    nchip = ngroup // 2
    nfar = nhead // 8
    vmem = pl.BlockSpec(memory_space=pltpu.VMEM)
    hbm = pl.BlockSpec(memory_space=pltpu.HBM)
    dma = pltpu.SemaphoreType.DMA
    operands = (
        sources.T,
        head_keep,
        enc_resid,
        enc_qkv,
        enc_bias,
        final_gain.reshape(chunks, LANES),
        cross_bias.T,
        out_weight,
        key_weight,
        value_weight,
        dec_query,
        out_grad,
    )
    held = pl.pallas_call(
        functools.partial(kernel, ngroup, nhead, mem),
        out_shape=(
            pltpu.VMEM((qrows, width), BF16),
            pltpu.VMEM((seq, dim), BF16),
        ),
        in_specs=[hbm] * 12,
        out_specs=(vmem, vmem),
        scratch_shapes=[
            pltpu.SMEM(sources.shape[::-1], jnp.int32),
            pltpu.SMEM(head_keep.shape, jnp.int32),
            pltpu.VMEM(enc_resid.shape, BF16),
            pltpu.VMEM(enc_qkv.shape, BF16),
            pltpu.VMEM(enc_bias.shape, F32),
            pltpu.VMEM((chunks, LANES), F32),
            pltpu.VMEM(cross_bias.shape[::-1], F32),
            pltpu.VMEM((ngroup,) + out_weight.shape, BF16),
            pltpu.VMEM((ngroup,) + key_weight.shape, BF16),
            pltpu.VMEM((ngroup,) + value_weight.shape, BF16),
            pltpu.VMEM((qrows, width), BF16),
            pltpu.VMEM((qrows, width), BF16),
            pltpu.VMEM((mem * seq * chunks, LANES), F32),
            pltpu.VMEM((seq * chunks, LANES), F32),
            pltpu.VMEM((nhead, blk, LANES), BF16),
            pltpu.VMEM((nhead - 1, blk, LANES), BF16),
            pltpu.VMEM((ngroup, blk, LANES), BF16),
            pltpu.VMEM((nhead, mem * blk, LANES), BF16),
            pltpu.VMEM((nhead, mem * blk, LANES), BF16),
            pltpu.VMEM((nfar, 7, mem * blk, LANES), BF16),
            pltpu.VMEM((nfar, mem * blk, LANES), BF16),
            pltpu.VMEM((nfar, mem * blk, LANES), BF16),
            pltpu.VMEM((width // DK, mem * seq, qrows), F32),
            pltpu.VMEM((ngroup * mem, blk, LANES), F32),
            pltpu.VMEM((ngroup, blk, LANES), BF16),
            pltpu.VMEM((ngroup - 1, blk, LANES), BF16),
            pltpu.VMEM((nhead, blk, LANES), BF16),
            dma((12,)),
            dma,
            dma((nchip,)),
            dma,
            dma,
            dma,
            dma((2, nchip)),
            dma,
            dma((2,)),
            dma((nfar,)),
            dma((nfar,)),
            dma((8,)),
            dma((6,)),
            pltpu.SemaphoreType.REGULAR,
        ],
        compiler_params=pltpu.CompilerParams(
            collective_id=0, has_side_effects=True, vmem_limit_bytes=40 * 1024 * 1024
        ),
    )(
        *(pltpu.with_memory_space_constraint(x, pltpu.HBM) for x in operands),
    )
    return tuple(
        pl.pallas_call(
            store,
            out_shape=tuple(pltpu.HBM(x.shape, x.dtype) for x in held),
            in_specs=[vmem, vmem],
            out_specs=(hbm, hbm),
            scratch_shapes=[dma((2,))],
        )(*(pltpu.with_memory_space_constraint(x, pltpu.VMEM) for x in held))
    )


def solution(mesh):
    in_specs = (
        P("group", None),
        P(None, "group", "head"),
        P(),
        P(("head", "group"), None),
        P(),
        P("group", "head"),
        P("group", "head"),
        P("group", "head"),
        P(),
        P("group", "head"),
        P(),
        P("group", "head"),
    )
    out_specs = (P("group", "head"), P("group", None))
    step = functools.partial(shards, mesh.shape["group"], mesh.shape["head"])
    return jax.shard_map(step, mesh=mesh, in_specs=in_specs, out_specs=out_specs, check_vma=False)
```

```python
import functools
import math

import jax
import jax.numpy as jnp
from jax import lax
from jax.experimental import pallas as pl
from jax.experimental.pallas import tpu as pltpu
from jax.sharding import PartitionSpec as P

MESH = pl.DeviceIdType.MESH
BF16 = jnp.bfloat16
F32 = jnp.float32
DK = 128
LANES = 128
EPS = 1e-06


def mm(a, b, ca, cb):
    return lax.dot_general(a, b, (((ca,), (cb,)), ((), ())), preferred_element_type=F32)


def kernel(
    ngroup,
    nhead,
    mem,
    sources_hbm,
    keep_hbm,
    resid_hbm,
    qkv_hbm,
    enc_bias_hbm,
    gain_hbm,
    cross_bias_hbm,
    out_w,
    key_w,
    value_w,
    query_hbm,
    grad_hbm,
    context,
    memory_grad,
    sources,
    keep,
    resid,
    qkv,
    enc_bias,
    gain,
    cross_bias,
    wo,
    kw,
    vw,
    query,
    grad,
    flat,
    resid_flat,
    out_send,
    out_recv,
    norm_all,
    norm_pick,
    dn_send,
    dn_near,
    dn_sum,
    dn_far,
    probs,
    pick,
    dn_out,
    dn_in,
    mg_all,
    local_sem,
    wo_send,
    wo_recv,
    wo_pass_send,
    wo_pass_recv,
    kv_send,
    kv_recv,
    kv_pass_send,
    kv_pass_recv,
    far_recv,
    near_recv,
    phase_send,
    phase_recv,
    ready,
):
    seq, dim = resid.shape
    width = query.shape[1]
    nheads = width // DK
    chunks = dim // LANES
    own_rows = seq // nhead
    blk = own_rows * chunks
    scale = 1.0 / math.sqrt(DK)
    g = lax.axis_index("group")
    h = lax.axis_index("head")
    core = lax.rem(g, 2)
    chip = lax.div(g, 2)
    sibling = g + 1 - 2 * core
    nchip = ngroup // 2

    nz, nx = nhead // 2, ngroup // 4
    z, y = lax.div(h, 2), lax.rem(h, 2)
    gx, gy = lax.div(g, 4), lax.rem(lax.div(g, 2), 2)

    def each(n, body):
        lax.fori_loop(1, n, lambda k, c: (body(k), c)[1], 0)

    def head_at(dz, dy):
        return lax.rem(z + dz + nz, nz) * 2 + lax.rem(y + dy, 2)

    def group_at(dx, dy, dc):
        return lax.rem(gx + dx, nx) * 4 + lax.rem(gy + dy, 2) * 2 + lax.rem(core + dc, 2)

    head_steps = sorted(
        [(dz, dy) for dz in range(nz) for dy in range(2)][1:], key=lambda t: -(min(t[0], nz - t[0]) * 2 + t[1])
    )

    def head_peer(k):
        j = lax.div(k - 1, 2)
        away = nz // 2 - lax.div(j + 1, 2)
        return head_at(away * (2 * lax.rem(j, 2) - 1), lax.rem(k, 2))

    def spread(dx, dy, dc):
        return -(min(dx, nx - dx) * 4 + dy * 4 + dc)

    steps = [(dx, dy, dc) for dx in range(nx) for dy in range(2) for dc in range(2)][1:]
    group_steps = sorted(steps, key=lambda t: spread(*t))
    chip_steps = [(dx, dy) for dx, dy, dc in group_steps if dc == 0]
    far_steps = sorted(range(2, nz, 4), key=lambda a: -min(a, nz - a))
    near_steps = [(2, 1), (1, 1), (nz - 1, 1), (0, 1), (2, 0), (1, 0), (nz - 1, 0)]

    def remote(src, dst, send, recv, where):
        return pltpu.make_async_remote_copy(
            src_ref=src,
            dst_ref=dst,
            send_sem=send,
            recv_sem=recv,
            device_id=where,
            device_id_type=MESH,
        )

    def total(ref, send, recv):
        return remote(ref, ref, send, recv, {"group": sibling})

    barrier = pltpu.get_barrier_semaphore()
    even, odd = g - core, g - core + 1

    def hello(**where):
        pl.semaphore_signal(barrier, inc=1, device_id=where, device_id_type=MESH)

    def tell_sibling():
        pl.semaphore_signal(ready, inc=1, device_id={"group": sibling}, device_id_type=MESH)

    each(nchip, lambda k: hello(group=lax.rem(chip + k, nchip) * 2))
    pl.when(core == 1)(lambda: hello(group=even))
    each(nhead, lambda k: hello(group=odd, head=head_peer(k)))
    locals_ = [
        pltpu.make_async_copy(query_hbm, query, local_sem.at[0]),
        pltpu.make_async_copy(grad_hbm, grad, local_sem.at[1]),
        pltpu.make_async_copy(out_w, wo.at[g], local_sem.at[2]),
        pltpu.make_async_copy(key_w, kw.at[g], local_sem.at[3]),
        pltpu.make_async_copy(value_w, vw.at[g], local_sem.at[4]),
        pltpu.make_async_copy(qkv_hbm, qkv, local_sem.at[5]),
        pltpu.make_async_copy(enc_bias_hbm, enc_bias, local_sem.at[6]),
        pltpu.make_async_copy(resid_hbm, resid, local_sem.at[7]),
        pltpu.make_async_copy(gain_hbm, gain, local_sem.at[8]),
        pltpu.make_async_copy(cross_bias_hbm, cross_bias, local_sem.at[9]),
        pltpu.make_async_copy(sources_hbm, sources, local_sem.at[10]),
        pltpu.make_async_copy(keep_hbm, keep, local_sem.at[11]),
    ]
    for copy in locals_:
        copy.start()

    @pl.when(core == 0)
    def _():
        pl.semaphore_wait(barrier, ngroup - 1)
        tell_sibling()

    @pl.when(core == 1)
    def _():
        pl.semaphore_wait(ready, 1)

    locals_[2].wait()
    for i, (dx, dy) in enumerate(chip_steps):
        remote(wo.at[g], wo.at[g], wo_send, wo_recv.at[i], {"group": group_at(dx, dy, 0)}).start()
    remote(wo.at[g], wo.at[g], wo_pass_send, wo_pass_recv, {"group": sibling}).start()

    locals_[3].wait()
    locals_[4].wait()
    locals_[5].wait()
    locals_[6].wait()
    bias = enc_bias[...]
    ctx = []
    for n in range(nheads):
        cols = slice(n * DK, (n + 1) * DK)
        scores = mm(qkv[0, :, cols], qkv[1, :, cols], 1, 1) * scale + bias
        e = jnp.exp(scores - jnp.max(scores, axis=1, keepdims=True))
        p = (e * (1.0 / jnp.sum(e, axis=1, keepdims=True))).astype(BF16)
        ctx.append(mm(p, qkv[2, :, cols], 1, 0).astype(BF16))
    ctx = jnp.concatenate(ctx, axis=1)

    def to_flat(x, ref, base):
        rows = x.shape[0]
        for c in range(chunks):
            ref[pl.ds(base * chunks + c, rows, stride=chunks), :] = x[:, c * LANES : (c + 1) * LANES]

    def from_flat(ref, base, rows, c):
        return ref[pl.ds(base * chunks + c, rows, stride=chunks), :]

    locals_[7].wait()
    to_flat(resid[...].astype(F32), resid_flat, 0)

    locals_[10].wait()
    for e in range(ngroup):
        for s in range(mem):
            reads = (sources[s, g] == e).astype(jnp.int32)
            pick[e * mem + s] = jnp.full((blk, LANES), reads, jnp.int32).astype(F32)

    for i, (dx, dy) in enumerate(chip_steps):
        there = wo.at[group_at(nx - dx, dy, 0)]
        remote(there, there, wo_send, wo_recv.at[i], {"group": sibling}).wait_recv()
        remote(there, there, wo_pass_send, wo_pass_recv, {"group": sibling}).start()

    @pl.when(core == 1)
    def _():
        pl.semaphore_wait(barrier, 2 * (nhead - 1))
        tell_sibling()

    total(wo.at[pl.ds(0, nchip)], wo_pass_send, wo_pass_recv).wait_recv()
    part = mm(ctx, wo[...].reshape(width, dim), 1, 0)

    to_flat(part, flat, 0)
    out_send[...] = flat[pl.ds(0, seq * chunks), :].reshape(nhead, blk, LANES).astype(BF16)

    @pl.when(core == 0)
    def _():
        pl.semaphore_wait(ready, 1)

    for i, step in enumerate(head_steps):
        there = head_at(*step)
        remote(out_send.at[there], out_recv.at[i], phase_send.at[0], phase_recv.at[0], {"head": there}).start()

    across = chip_steps.index((0, 1))
    along = [(i, dx) for i, (dx, dy) in enumerate(chip_steps) if dy == 0]

    def send_weight(j, ref):
        there = ref.at[g]
        remote(there, there, kv_send, kv_recv.at[j, across], {"group": group_at(0, 1, 0)}).start()
        for i, dx in along:
            remote(there, there, kv_send, kv_recv.at[j, i], {"group": group_at(dx, 0, 0)}).start()
        remote(there, there, kv_pass_send, kv_pass_recv.at[j], {"group": sibling}).start()

    def relay_weight(j, ref):
        there = ref.at[group_at(0, 1, 0)]
        remote(there, there, kv_send, kv_recv.at[j, across], {"group": sibling}).wait_recv()
        for _, dx in along:
            i = chip_steps.index((dx, 1))
            remote(there, there, kv_send, kv_recv.at[j, i], {"group": group_at(dx, 0, 0)}).start()
        remote(there, there, kv_pass_send, kv_pass_recv.at[j], {"group": sibling}).start()

    send_weight(0, kw)
    relay_weight(0, kw)

    mine = pl.ds(pl.multiple_of(h * blk, blk), blk)
    memory = flat[mine, :] + resid_flat[mine, :]
    total(out_recv, phase_send.at[0], phase_recv.at[0]).wait_recv()
    memory = memory + jnp.sum(out_recv[...].astype(F32), axis=0)

    def row_mean(x):
        x3 = x.reshape(own_rows, chunks, LANES)
        m = jnp.sum(jnp.sum(x3, axis=1, keepdims=True), axis=2, keepdims=True) * (1.0 / dim)
        return jnp.broadcast_to(m, x3.shape).reshape(blk, LANES)

    locals_[8].wait()
    gains = jnp.broadcast_to(gain[...][None], (own_rows, chunks, LANES)).reshape(blk, LANES)
    inv = lax.rsqrt(row_mean(memory * memory) + EPS)
    normed = memory * inv
    norm_all[g] = (normed * gains).astype(BF16)

    there = norm_all.at[g]
    for step in group_steps:
        remote(there, there, phase_send.at[1], phase_recv.at[1], {"group": group_at(*step)}).start()
    total(norm_all.at[pl.ds(0, ngroup - 1)], phase_send.at[1], phase_recv.at[1]).wait_recv()

    for s in range(mem):
        norm_pick[h, s * blk : (s + 1) * blk, :] = norm_all[sources[s, g]]

    there = norm_pick.at[h]
    for i, a in enumerate(far_steps):
        remote(there, there, phase_send.at[2], far_recv.at[i], {"head": head_at(a, 0)}).start()
    send_weight(1, vw)

    def pass_kv(j, ref):
        for i, (dx, dy) in enumerate(chip_steps):
            if i == across:
                continue
            there = ref.at[group_at(nx - dx, dy, 0)]
            remote(there, there, kv_send, kv_recv.at[j, i], {"group": sibling}).wait_recv()
            remote(there, there, kv_pass_send, kv_pass_recv.at[j], {"group": sibling}).start()

    pass_kv(0, kw)

    relay_weight(1, vw)

    nfar = len(far_steps)
    npass = nfar * len(near_steps) - 1
    for i, a in reversed(list(enumerate(far_steps))):
        there = norm_pick.at[head_at(nz - a, 0)]
        remote(there, there, phase_send.at[2], far_recv.at[i], {"head": head_at(a, 0)}).wait_recv()
        for b, dy in near_steps:
            if (a + b) % nz or dy:
                remote(there, there, phase_send.at[6], phase_recv.at[2], {"head": head_at(b, dy)}).start()
    pass_kv(1, vw)
    for i in (0, 9, 11):
        locals_[i].wait()
    total(kw.at[pl.ds(0, nchip)], kv_pass_send, kv_pass_recv.at[0]).wait_recv()
    total(norm_pick.at[pl.ds(0, npass)], phase_send.at[6], phase_recv.at[2]).wait_recv()
    for s in range(mem):
        rows = norm_pick[:, s * blk : (s + 1) * blk, :].astype(F32).reshape(seq * chunks, LANES)
        flat[pl.ds(s * seq * chunks, seq * chunks), :] = rows
    rows = mem * seq
    picked = jnp.concatenate([from_flat(flat, 0, rows, c).astype(BF16) for c in range(chunks)], axis=1)

    key_full = kw[...].reshape(dim, width)
    keys = mm(picked, key_full, 1, 0).astype(BF16)
    cbias = cross_bias[...]
    qrows = query.shape[0]
    for n in range(nheads):
        cols = slice(n * DK, (n + 1) * DK)
        cross = (mm(keys[:, cols], query[:, cols], 1, 1) * scale).reshape(mem, seq, qrows) + cbias[None]
        cross = cross.reshape(rows, qrows)
        e = jnp.exp(cross - jnp.max(cross, axis=0, keepdims=True))
        probs[n] = e * (1.0 / jnp.sum(e, axis=0, keepdims=True))

    locals_[1].wait()
    total(vw.at[pl.ds(0, nchip)], kv_pass_send, kv_pass_recv.at[1]).wait_recv()
    value_full = vw[...].reshape(dim, width)
    values = mm(picked, value_full, 1, 0).astype(BF16)
    dks, dvs = [], []
    for n in range(nheads):
        cols = slice(n * DK, (n + 1) * DK)
        kept = keep[0, n].astype(F32)
        q_n, g_n, v_n = query[:, cols], grad[:, cols], values[:, cols]
        prob = probs[n]
        prob_low = prob.astype(BF16)
        context[:, cols] = (mm(prob_low, v_n, 0, 0) * kept).astype(BF16)
        dprob = mm(v_n, g_n, 1, 1)
        delta = jnp.sum(prob * dprob, axis=0, keepdims=True)
        dscore = (prob * (dprob - delta) * (scale * kept)).astype(BF16)
        dks.append(mm(dscore, q_n, 1, 0).astype(BF16))
        dvs.append((mm(prob_low, g_n, 1, 0) * kept).astype(BF16))
    dks = jnp.concatenate(dks, axis=1)
    dvs = jnp.concatenate(dvs, axis=1)
    dnorm = mm(dks, key_full, 1, 1) + mm(dvs, value_full, 1, 1)

    to_flat(dnorm, flat, 0)
    for s in range(mem):
        block = flat[pl.ds(s * seq * chunks, seq * chunks), :].reshape(nhead, blk, LANES)
        dn_send[:, s * blk : (s + 1) * blk, :] = block.astype(BF16)

    for i, a in enumerate(far_steps):
        for j, (b, dy) in enumerate(near_steps):
            there = dn_send.at[head_at(a + b, dy)]
            remote(there, dn_near.at[i, j], phase_send.at[3], near_recv.at[i], {"head": head_at(b, dy)}).start()
    for i, a in enumerate(far_steps):
        total(dn_near.at[i], phase_send.at[3], near_recv.at[i]).wait_recv()
        near = dn_send[head_at(a, 0)].astype(F32) + jnp.sum(dn_near[i].astype(F32), axis=0)
        dn_sum[i] = near.astype(BF16)
        remote(dn_sum.at[i], dn_far.at[i], phase_send.at[7], phase_recv.at[3], {"head": head_at(a, 0)}).start()
    total(dn_far, phase_send.at[7], phase_recv.at[3]).wait_recv()
    dn_sum_all = jnp.sum(dn_far[...].astype(F32), axis=0)

    for e in range(ngroup):
        acc = jnp.zeros((blk, LANES), F32)
        for s in range(mem):
            acc = acc + dn_sum_all[s * blk : (s + 1) * blk] * pick[e * mem + s]
        dn_out[e] = acc.astype(BF16)
    for i, step in enumerate(group_steps):
        there = group_at(*step)
        remote(dn_out.at[there], dn_in.at[i], phase_send.at[4], phase_recv.at[4], {"group": there}).start()
    acc = dn_out[g].astype(F32)
    total(dn_in, phase_send.at[4], phase_recv.at[4]).wait_recv()
    acc = acc + jnp.sum(dn_in[...].astype(F32), axis=0)
    scaled = acc * gains
    mg_all[h] = (inv * (scaled - normed * row_mean(scaled * normed))).astype(BF16)

    there = mg_all.at[h]
    for step in head_steps:
        remote(there, there, phase_send.at[5], phase_recv.at[5], {"head": head_at(*step)}).start()
    total(mg_all.at[pl.ds(0, nhead - 1)], phase_send.at[5], phase_recv.at[5]).wait_recv()
    flat[pl.ds(0, seq * chunks), :] = mg_all[...].astype(F32).reshape(seq * chunks, LANES)
    for c in range(chunks):
        memory_grad[:, c * LANES : (c + 1) * LANES] = from_flat(flat, 0, seq, c).astype(BF16)

    total(wo.at[pl.ds(0, nchip - 1)], wo_send, wo_recv.at[0]).wait_send()
    total(wo.at[pl.ds(0, nchip)], wo_pass_send, wo_pass_recv).wait_send()
    total(kw.at[pl.ds(0, 2 * nchip - 2)], kv_send, kv_recv.at[0, 0]).wait_send()
    total(kw.at[pl.ds(0, 2 * nchip)], kv_pass_send, kv_pass_recv.at[0]).wait_send()
    sent = (
        out_recv,
        norm_all.at[pl.ds(0, ngroup - 1)],
        norm_pick.at[pl.ds(0, nfar)],
        dn_near,
        dn_in,
        mg_all.at[pl.ds(0, nhead - 1)],
        norm_pick.at[pl.ds(0, npass)],
        dn_far,
    )
    for i, ref in enumerate(sent):
        total(ref, phase_send.at[i], phase_recv.at[0]).wait_send()


def store(context, memory_grad, context_hbm, memory_grad_hbm, sem):
    copies = (
        pltpu.make_async_copy(context, context_hbm, sem.at[0]),
        pltpu.make_async_copy(memory_grad, memory_grad_hbm, sem.at[1]),
    )
    for copy in copies:
        copy.start()
    for copy in copies:
        copy.wait()


def shards(
    ngroup,
    nhead,
    enc_resid,
    enc_qkv,
    enc_bias,
    out_weight,
    final_gain,
    key_weight,
    value_weight,
    dec_query,
    cross_bias,
    out_grad,
    sources,
    head_keep,
):
    seq, dim = enc_resid.shape
    qrows, width = dec_query.shape
    mem = sources.shape[1]
    chunks = dim // LANES
    blk = seq // nhead * chunks
    nchip = ngroup // 2
    nfar = nhead // 8
    vmem = pl.BlockSpec(memory_space=pltpu.VMEM)
    hbm = pl.BlockSpec(memory_space=pltpu.HBM)
    dma = pltpu.SemaphoreType.DMA
    operands = (
        sources.T,
        head_keep,
        enc_resid,
        enc_qkv,
        enc_bias,
        final_gain.reshape(chunks, LANES),
        cross_bias.T,
        out_weight,
        key_weight,
        value_weight,
        dec_query,
        out_grad,
    )
    held = pl.pallas_call(
        functools.partial(kernel, ngroup, nhead, mem),
        out_shape=(
            pltpu.VMEM((qrows, width), BF16),
            pltpu.VMEM((seq, dim), BF16),
        ),
        in_specs=[hbm] * 12,
        out_specs=(vmem, vmem),
        scratch_shapes=[
            pltpu.SMEM(sources.shape[::-1], jnp.int32),
            pltpu.SMEM(head_keep.shape, jnp.int32),
            pltpu.VMEM(enc_resid.shape, BF16),
            pltpu.VMEM(enc_qkv.shape, BF16),
            pltpu.VMEM(enc_bias.shape, F32),
            pltpu.VMEM((chunks, LANES), F32),
            pltpu.VMEM(cross_bias.shape[::-1], F32),
            pltpu.VMEM((ngroup,) + out_weight.shape, BF16),
            pltpu.VMEM((ngroup,) + key_weight.shape, BF16),
            pltpu.VMEM((ngroup,) + value_weight.shape, BF16),
            pltpu.VMEM((qrows, width), BF16),
            pltpu.VMEM((qrows, width), BF16),
            pltpu.VMEM((mem * seq * chunks, LANES), F32),
            pltpu.VMEM((seq * chunks, LANES), F32),
            pltpu.VMEM((nhead, blk, LANES), BF16),
            pltpu.VMEM((nhead - 1, blk, LANES), BF16),
            pltpu.VMEM((ngroup, blk, LANES), BF16),
            pltpu.VMEM((nhead, mem * blk, LANES), BF16),
            pltpu.VMEM((nhead, mem * blk, LANES), BF16),
            pltpu.VMEM((nfar, 7, mem * blk, LANES), BF16),
            pltpu.VMEM((nfar, mem * blk, LANES), BF16),
            pltpu.VMEM((nfar, mem * blk, LANES), BF16),
            pltpu.VMEM((width // DK, mem * seq, qrows), F32),
            pltpu.VMEM((ngroup * mem, blk, LANES), F32),
            pltpu.VMEM((ngroup, blk, LANES), BF16),
            pltpu.VMEM((ngroup - 1, blk, LANES), BF16),
            pltpu.VMEM((nhead, blk, LANES), BF16),
            dma((12,)),
            dma,
            dma((nchip,)),
            dma,
            dma,
            dma,
            dma((2, nchip)),
            dma,
            dma((2,)),
            dma((nfar,)),
            dma((nfar,)),
            dma((8,)),
            dma((6,)),
            pltpu.SemaphoreType.REGULAR,
        ],
        compiler_params=pltpu.CompilerParams(
            collective_id=0, has_side_effects=True, vmem_limit_bytes=40 * 1024 * 1024
        ),
    )(
        *(pltpu.with_memory_space_constraint(x, pltpu.HBM) for x in operands),
    )
    return tuple(
        pl.pallas_call(
            store,
            out_shape=tuple(pltpu.HBM(x.shape, x.dtype) for x in held),
            in_specs=[vmem, vmem],
            out_specs=(hbm, hbm),
            scratch_shapes=[dma((2,))],
        )(*(pltpu.with_memory_space_constraint(x, pltpu.VMEM) for x in held))
    )


def solution(mesh):
    in_specs = (
        P("group", None),
        P(None, "group", "head"),
        P(),
        P(("head", "group"), None),
        P(),
        P("group", "head"),
        P("group", "head"),
        P("group", "head"),
        P(),
        P("group", "head"),
        P(),
        P("group", "head"),
    )
    out_specs = (P("group", "head"), P("group", None))
    step = functools.partial(shards, mesh.shape["group"], mesh.shape["head"])
    return jax.shard_map(step, mesh=mesh, in_specs=in_specs, out_specs=out_specs, check_vma=False)
```

```python
import functools
import math

import jax
import jax.numpy as jnp
from jax import lax
from jax.experimental import pallas as pl
from jax.experimental.pallas import tpu as pltpu
from jax.sharding import PartitionSpec as P

MESH = pl.DeviceIdType.MESH
BF16 = jnp.bfloat16
F32 = jnp.float32
DK = 128
LANES = 128
EPS = 1e-06


def mm(a, b, ca, cb):
    return lax.dot_general(a, b, (((ca,), (cb,)), ((), ())), preferred_element_type=F32)


def kernel(
    ngroup,
    nhead,
    mem,
    sources_hbm,
    keep_hbm,
    resid_hbm,
    qkv_hbm,
    enc_bias_hbm,
    gain_hbm,
    cross_bias_hbm,
    out_w,
    key_w,
    value_w,
    query_hbm,
    grad_hbm,
    context,
    memory_grad,
    sources,
    keep,
    resid,
    qkv,
    enc_bias,
    gain,
    cross_bias,
    wo,
    kw,
    vw,
    query,
    grad,
    flat,
    resid_flat,
    out_send,
    out_recv,
    norm_all,
    norm_pick,
    dn_send,
    dn_near,
    dn_sum,
    dn_far,
    probs,
    pick,
    dn_out,
    dn_in,
    mg_all,
    local_sem,
    wo_send,
    wo_recv,
    wo_pass_send,
    wo_pass_recv,
    kv_send,
    kv_recv,
    kv_pass_send,
    kv_pass_recv,
    far_recv,
    near_recv,
    phase_send,
    phase_recv,
    ready,
):
    seq, dim = resid.shape
    width = query.shape[1]
    nheads = width // DK
    chunks = dim // LANES
    own_rows = seq // nhead
    blk = own_rows * chunks
    scale = 1.0 / math.sqrt(DK)
    g = lax.axis_index("group")
    h = lax.axis_index("head")
    core = lax.rem(g, 2)
    chip = lax.div(g, 2)
    sibling = g + 1 - 2 * core
    nchip = ngroup // 2

    nz, nx = nhead // 2, ngroup // 4
    z, y = lax.div(h, 2), lax.rem(h, 2)
    gx, gy = lax.div(g, 4), lax.rem(lax.div(g, 2), 2)

    def each(n, body):
        lax.fori_loop(1, n, lambda k, c: (body(k), c)[1], 0)

    def head_at(dz, dy):
        return lax.rem(z + dz + nz, nz) * 2 + lax.rem(y + dy, 2)

    def group_at(dx, dy, dc):
        return lax.rem(gx + dx, nx) * 4 + lax.rem(gy + dy, 2) * 2 + lax.rem(core + dc, 2)

    head_steps = sorted(
        [(dz, dy) for dz in range(nz) for dy in range(2)][1:], key=lambda t: -(min(t[0], nz - t[0]) * 2 + t[1])
    )

    def head_peer(k):
        j = lax.div(k - 1, 2)
        away = nz // 2 - lax.div(j + 1, 2)
        return head_at(away * (2 * lax.rem(j, 2) - 1), lax.rem(k, 2))

    def spread(dx, dy, dc):
        return -(min(dx, nx - dx) * 4 + dy * 4 + dc)

    steps = [(dx, dy, dc) for dx in range(nx) for dy in range(2) for dc in range(2)][1:]
    group_steps = sorted(steps, key=lambda t: spread(*t))
    chip_steps = [(dx, dy) for dx, dy, dc in group_steps if dc == 0]
    far_steps = sorted(range(2, nz, 4), key=lambda a: -min(a, nz - a))
    near_steps = [(2, 1), (1, 1), (nz - 1, 1), (0, 1), (2, 0), (1, 0), (nz - 1, 0)]

    def remote(src, dst, send, recv, where):
        return pltpu.make_async_remote_copy(
            src_ref=src,
            dst_ref=dst,
            send_sem=send,
            recv_sem=recv,
            device_id=where,
            device_id_type=MESH,
        )

    def total(ref, send, recv):
        return remote(ref, ref, send, recv, {"group": sibling})

    barrier = pltpu.get_barrier_semaphore()
    even, odd = g - core, g - core + 1

    def hello(**where):
        pl.semaphore_signal(barrier, inc=1, device_id=where, device_id_type=MESH)

    def tell_sibling():
        pl.semaphore_signal(ready, inc=1, device_id={"group": sibling}, device_id_type=MESH)

    each(nchip, lambda k: hello(group=lax.rem(chip + k, nchip) * 2))
    pl.when(core == 1)(lambda: hello(group=even))
    for step in head_steps:
        hello(group=odd, head=head_at(*step))
    locals_ = [
        pltpu.make_async_copy(query_hbm, query, local_sem.at[0]),
        pltpu.make_async_copy(grad_hbm, grad, local_sem.at[1]),
        pltpu.make_async_copy(out_w, wo.at[g], local_sem.at[2]),
        pltpu.make_async_copy(key_w, kw.at[g], local_sem.at[3]),
        pltpu.make_async_copy(value_w, vw.at[g], local_sem.at[4]),
        pltpu.make_async_copy(qkv_hbm, qkv, local_sem.at[5]),
        pltpu.make_async_copy(enc_bias_hbm, enc_bias, local_sem.at[6]),
        pltpu.make_async_copy(resid_hbm, resid, local_sem.at[7]),
        pltpu.make_async_copy(gain_hbm, gain, local_sem.at[8]),
        pltpu.make_async_copy(cross_bias_hbm, cross_bias, local_sem.at[9]),
        pltpu.make_async_copy(sources_hbm, sources, local_sem.at[10]),
        pltpu.make_async_copy(keep_hbm, keep, local_sem.at[11]),
    ]
    for copy in locals_:
        copy.start()

    @pl.when(core == 0)
    def _():
        pl.semaphore_wait(barrier, ngroup - 1)
        tell_sibling()

    @pl.when(core == 1)
    def _():
        pl.semaphore_wait(ready, 1)

    locals_[2].wait()
    for i, (dx, dy) in enumerate(chip_steps):
        remote(wo.at[g], wo.at[g], wo_send, wo_recv.at[i], {"group": group_at(dx, dy, 0)}).start()
    remote(wo.at[g], wo.at[g], wo_pass_send, wo_pass_recv, {"group": sibling}).start()

    locals_[3].wait()
    locals_[4].wait()
    locals_[5].wait()
    locals_[6].wait()
    bias = enc_bias[...]
    ctx = []
    for n in range(nheads):
        cols = slice(n * DK, (n + 1) * DK)
        scores = mm(qkv[0, :, cols], qkv[1, :, cols], 1, 1) * scale + bias
        e = jnp.exp(scores - jnp.max(scores, axis=1, keepdims=True))
        p = (e * (1.0 / jnp.sum(e, axis=1, keepdims=True))).astype(BF16)
        ctx.append(mm(p, qkv[2, :, cols], 1, 0).astype(BF16))
    ctx = jnp.concatenate(ctx, axis=1)

    def to_flat(x, ref, base):
        rows = x.shape[0]
        for c in range(chunks):
            ref[pl.ds(base * chunks + c, rows, stride=chunks), :] = x[:, c * LANES : (c + 1) * LANES]

    def from_flat(ref, base, rows, c):
        return ref[pl.ds(base * chunks + c, rows, stride=chunks), :]

    locals_[7].wait()
    to_flat(resid[...].astype(F32), resid_flat, 0)

    locals_[10].wait()
    for e in range(ngroup):
        for s in range(mem):
            reads = (sources[s, g] == e).astype(jnp.int32)
            pick[e * mem + s] = jnp.full((blk, LANES), reads, jnp.int32).astype(F32)

    for i, (dx, dy) in enumerate(chip_steps):
        there = wo.at[group_at(nx - dx, dy, 0)]
        remote(there, there, wo_send, wo_recv.at[i], {"group": sibling}).wait_recv()
        remote(there, there, wo_pass_send, wo_pass_recv, {"group": sibling}).start()

    @pl.when(core == 1)
    def _():
        pl.semaphore_wait(barrier, 2 * (nhead - 1))
        tell_sibling()

    total(wo.at[pl.ds(0, nchip)], wo_pass_send, wo_pass_recv).wait_recv()
    part = mm(ctx, wo[...].reshape(width, dim), 1, 0)

    to_flat(part, flat, 0)
    out_send[...] = flat[pl.ds(0, seq * chunks), :].reshape(nhead, blk, LANES).astype(BF16)

    @pl.when(core == 0)
    def _():
        pl.semaphore_wait(ready, 1)

    for i, step in enumerate(head_steps):
        there = head_at(*step)
        remote(out_send.at[there], out_recv.at[i], phase_send.at[0], phase_recv.at[0], {"head": there}).start()

    across = chip_steps.index((0, 1))
    along = [(i, dx) for i, (dx, dy) in enumerate(chip_steps) if dy == 0]

    def send_weight(j, ref):
        there = ref.at[g]
        remote(there, there, kv_send, kv_recv.at[j, across], {"group": group_at(0, 1, 0)}).start()
        for i, dx in along:
            remote(there, there, kv_send, kv_recv.at[j, i], {"group": group_at(dx, 0, 0)}).start()
        remote(there, there, kv_pass_send, kv_pass_recv.at[j], {"group": sibling}).start()

    def relay_weight(j, ref):
        there = ref.at[group_at(0, 1, 0)]
        remote(there, there, kv_send, kv_recv.at[j, across], {"group": sibling}).wait_recv()
        for _, dx in along:
            i = chip_steps.index((dx, 1))
            remote(there, there, kv_send, kv_recv.at[j, i], {"group": group_at(dx, 0, 0)}).start()
        remote(there, there, kv_pass_send, kv_pass_recv.at[j], {"group": sibling}).start()

    def pass_kv(j, ref):
        for i, (dx, dy) in enumerate(chip_steps):
            if i == across:
                continue
            there = ref.at[group_at(nx - dx, dy, 0)]
            remote(there, there, kv_send, kv_recv.at[j, i], {"group": sibling}).wait_recv()
            remote(there, there, kv_pass_send, kv_pass_recv.at[j], {"group": sibling}).start()

    send_weight(0, kw)
    relay_weight(0, kw)

    mine = pl.ds(pl.multiple_of(h * blk, blk), blk)
    memory = flat[mine, :] + resid_flat[mine, :]
    total(out_recv, phase_send.at[0], phase_recv.at[0]).wait_recv()
    memory = memory + jnp.sum(out_recv[...].astype(F32), axis=0)

    def row_mean(x):
        x3 = x.reshape(own_rows, chunks, LANES)
        m = jnp.sum(jnp.sum(x3, axis=1, keepdims=True), axis=2, keepdims=True) * (1.0 / dim)
        return jnp.broadcast_to(m, x3.shape).reshape(blk, LANES)

    locals_[8].wait()
    gains = jnp.broadcast_to(gain[...][None], (own_rows, chunks, LANES)).reshape(blk, LANES)
    inv = lax.rsqrt(row_mean(memory * memory) + EPS)
    normed = memory * inv
    norm_all[g] = (normed * gains).astype(BF16)

    there = norm_all.at[g]
    for step in group_steps:
        remote(there, there, phase_send.at[1], phase_recv.at[1], {"group": group_at(*step)}).start()
    pass_kv(0, kw)
    total(norm_all.at[pl.ds(0, ngroup - 1)], phase_send.at[1], phase_recv.at[1]).wait_recv()

    for s in range(mem):
        norm_pick[h, s * blk : (s + 1) * blk, :] = norm_all[sources[s, g]]

    there = norm_pick.at[h]
    for i, a in enumerate(far_steps):
        remote(there, there, phase_send.at[2], far_recv.at[i], {"head": head_at(a, 0)}).start()
    send_weight(1, vw)

    relay_weight(1, vw)

    nfar = len(far_steps)
    npass = nfar * len(near_steps) - 1
    for i, a in reversed(list(enumerate(far_steps))):
        there = norm_pick.at[head_at(nz - a, 0)]
        remote(there, there, phase_send.at[2], far_recv.at[i], {"head": head_at(a, 0)}).wait_recv()
        for b, dy in near_steps:
            if (a + b) % nz or dy:
                remote(there, there, phase_send.at[6], phase_recv.at[2], {"head": head_at(b, dy)}).start()
    pass_kv(1, vw)
    for i in (0, 9, 11):
        locals_[i].wait()
    total(kw.at[pl.ds(0, nchip)], kv_pass_send, kv_pass_recv.at[0]).wait_recv()
    total(norm_pick.at[pl.ds(0, npass)], phase_send.at[6], phase_recv.at[2]).wait_recv()
    for s in range(mem):
        rows = norm_pick[:, s * blk : (s + 1) * blk, :].astype(F32).reshape(seq * chunks, LANES)
        flat[pl.ds(s * seq * chunks, seq * chunks), :] = rows
    rows = mem * seq
    picked = jnp.concatenate([from_flat(flat, 0, rows, c).astype(BF16) for c in range(chunks)], axis=1)

    key_full = kw[...].reshape(dim, width)
    keys = mm(picked, key_full, 1, 0).astype(BF16)
    cbias = cross_bias[...]
    qrows = query.shape[0]
    for n in range(nheads):
        cols = slice(n * DK, (n + 1) * DK)
        cross = (mm(keys[:, cols], query[:, cols], 1, 1) * scale).reshape(mem, seq, qrows) + cbias[None]
        cross = cross.reshape(rows, qrows)
        e = jnp.exp(cross - jnp.max(cross, axis=0, keepdims=True))
        probs[n] = e * (1.0 / jnp.sum(e, axis=0, keepdims=True))

    locals_[1].wait()
    total(vw.at[pl.ds(0, nchip)], kv_pass_send, kv_pass_recv.at[1]).wait_recv()
    value_full = vw[...].reshape(dim, width)
    values = mm(picked, value_full, 1, 0).astype(BF16)
    dks, dvs = [], []
    for n in range(nheads):
        cols = slice(n * DK, (n + 1) * DK)
        kept = keep[0, n].astype(F32)
        q_n, g_n, v_n = query[:, cols], grad[:, cols], values[:, cols]
        prob = probs[n]
        prob_low = prob.astype(BF16)
        context[:, cols] = (mm(prob_low, v_n, 0, 0) * kept).astype(BF16)
        dprob = mm(v_n, g_n, 1, 1)
        delta = jnp.sum(prob * dprob, axis=0, keepdims=True)
        dscore = (prob * (dprob - delta) * (scale * kept)).astype(BF16)
        dks.append(mm(dscore, q_n, 1, 0).astype(BF16))
        dvs.append((mm(prob_low, g_n, 1, 0) * kept).astype(BF16))
    dks = jnp.concatenate(dks, axis=1)
    dvs = jnp.concatenate(dvs, axis=1)
    dnorm = mm(dks, key_full, 1, 1) + mm(dvs, value_full, 1, 1)

    to_flat(dnorm, flat, 0)
    for s in range(mem):
        block = flat[pl.ds(s * seq * chunks, seq * chunks), :].reshape(nhead, blk, LANES)
        dn_send[:, s * blk : (s + 1) * blk, :] = block.astype(BF16)

    for i, a in enumerate(far_steps):
        for j, (b, dy) in enumerate(near_steps):
            there = dn_send.at[head_at(a + b, dy)]
            remote(there, dn_near.at[i, j], phase_send.at[3], near_recv.at[i], {"head": head_at(b, dy)}).start()
    for i, a in enumerate(far_steps):
        total(dn_near.at[i], phase_send.at[3], near_recv.at[i]).wait_recv()
        near = dn_send[head_at(a, 0)].astype(F32) + jnp.sum(dn_near[i].astype(F32), axis=0)
        dn_sum[i] = near.astype(BF16)
        remote(dn_sum.at[i], dn_far.at[i], phase_send.at[7], phase_recv.at[3], {"head": head_at(a, 0)}).start()
    total(dn_far, phase_send.at[7], phase_recv.at[3]).wait_recv()
    dn_sum_all = jnp.sum(dn_far[...].astype(F32), axis=0)

    for e in range(ngroup):
        acc = jnp.zeros((blk, LANES), F32)
        for s in range(mem):
            acc = acc + dn_sum_all[s * blk : (s + 1) * blk] * pick[e * mem + s]
        dn_out[e] = acc.astype(BF16)
    for i, step in enumerate(group_steps):
        there = group_at(*step)
        remote(dn_out.at[there], dn_in.at[i], phase_send.at[4], phase_recv.at[4], {"group": there}).start()
    acc = dn_out[g].astype(F32)
    total(dn_in, phase_send.at[4], phase_recv.at[4]).wait_recv()
    acc = acc + jnp.sum(dn_in[...].astype(F32), axis=0)
    scaled = acc * gains
    mg_all[h] = (inv * (scaled - normed * row_mean(scaled * normed))).astype(BF16)

    there = mg_all.at[h]
    for step in head_steps:
        remote(there, there, phase_send.at[5], phase_recv.at[5], {"head": head_at(*step)}).start()
    total(mg_all.at[pl.ds(0, nhead - 1)], phase_send.at[5], phase_recv.at[5]).wait_recv()
    flat[pl.ds(0, seq * chunks), :] = mg_all[...].astype(F32).reshape(seq * chunks, LANES)
    for c in range(chunks):
        memory_grad[:, c * LANES : (c + 1) * LANES] = from_flat(flat, 0, seq, c).astype(BF16)

    total(wo.at[pl.ds(0, nchip - 1)], wo_send, wo_recv.at[0]).wait_send()
    total(wo.at[pl.ds(0, nchip)], wo_pass_send, wo_pass_recv).wait_send()
    total(kw.at[pl.ds(0, 2 * nchip - 2)], kv_send, kv_recv.at[0, 0]).wait_send()
    total(kw.at[pl.ds(0, 2 * nchip)], kv_pass_send, kv_pass_recv.at[0]).wait_send()
    sent = (
        out_recv,
        norm_all.at[pl.ds(0, ngroup - 1)],
        norm_pick.at[pl.ds(0, nfar)],
        dn_near,
        dn_in,
        mg_all.at[pl.ds(0, nhead - 1)],
        norm_pick.at[pl.ds(0, npass)],
        dn_far,
    )
    for i, ref in enumerate(sent):
        total(ref, phase_send.at[i], phase_recv.at[0]).wait_send()


def store(context, memory_grad, context_hbm, memory_grad_hbm, sem):
    copies = (
        pltpu.make_async_copy(context, context_hbm, sem.at[0]),
        pltpu.make_async_copy(memory_grad, memory_grad_hbm, sem.at[1]),
    )
    for copy in copies:
        copy.start()
    for copy in copies:
        copy.wait()


def shards(
    ngroup,
    nhead,
    enc_resid,
    enc_qkv,
    enc_bias,
    out_weight,
    final_gain,
    key_weight,
    value_weight,
    dec_query,
    cross_bias,
    out_grad,
    sources,
    head_keep,
):
    seq, dim = enc_resid.shape
    qrows, width = dec_query.shape
    mem = sources.shape[1]
    chunks = dim // LANES
    blk = seq // nhead * chunks
    nchip = ngroup // 2
    nfar = nhead // 8
    vmem = pl.BlockSpec(memory_space=pltpu.VMEM)
    hbm = pl.BlockSpec(memory_space=pltpu.HBM)
    dma = pltpu.SemaphoreType.DMA
    operands = (
        sources.T,
        head_keep,
        enc_resid,
        enc_qkv,
        enc_bias,
        final_gain.reshape(chunks, LANES),
        cross_bias.T,
        out_weight,
        key_weight,
        value_weight,
        dec_query,
        out_grad,
    )
    held = pl.pallas_call(
        functools.partial(kernel, ngroup, nhead, mem),
        out_shape=(
            pltpu.VMEM((qrows, width), BF16),
            pltpu.VMEM((seq, dim), BF16),
        ),
        in_specs=[hbm] * 12,
        out_specs=(vmem, vmem),
        scratch_shapes=[
            pltpu.SMEM(sources.shape[::-1], jnp.int32),
            pltpu.SMEM(head_keep.shape, jnp.int32),
            pltpu.VMEM(enc_resid.shape, BF16),
            pltpu.VMEM(enc_qkv.shape, BF16),
            pltpu.VMEM(enc_bias.shape, F32),
            pltpu.VMEM((chunks, LANES), F32),
            pltpu.VMEM(cross_bias.shape[::-1], F32),
            pltpu.VMEM((ngroup,) + out_weight.shape, BF16),
            pltpu.VMEM((ngroup,) + key_weight.shape, BF16),
            pltpu.VMEM((ngroup,) + value_weight.shape, BF16),
            pltpu.VMEM((qrows, width), BF16),
            pltpu.VMEM((qrows, width), BF16),
            pltpu.VMEM((mem * seq * chunks, LANES), F32),
            pltpu.VMEM((seq * chunks, LANES), F32),
            pltpu.VMEM((nhead, blk, LANES), BF16),
            pltpu.VMEM((nhead - 1, blk, LANES), BF16),
            pltpu.VMEM((ngroup, blk, LANES), BF16),
            pltpu.VMEM((nhead, mem * blk, LANES), BF16),
            pltpu.VMEM((nhead, mem * blk, LANES), BF16),
            pltpu.VMEM((nfar, 7, mem * blk, LANES), BF16),
            pltpu.VMEM((nfar, mem * blk, LANES), BF16),
            pltpu.VMEM((nfar, mem * blk, LANES), BF16),
            pltpu.VMEM((width // DK, mem * seq, qrows), F32),
            pltpu.VMEM((ngroup * mem, blk, LANES), F32),
            pltpu.VMEM((ngroup, blk, LANES), BF16),
            pltpu.VMEM((ngroup - 1, blk, LANES), BF16),
            pltpu.VMEM((nhead, blk, LANES), BF16),
            dma((12,)),
            dma,
            dma((nchip,)),
            dma,
            dma,
            dma,
            dma((2, nchip)),
            dma,
            dma((2,)),
            dma((nfar,)),
            dma((nfar,)),
            dma((8,)),
            dma((6,)),
            pltpu.SemaphoreType.REGULAR,
        ],
        compiler_params=pltpu.CompilerParams(
            collective_id=0, has_side_effects=True, vmem_limit_bytes=40 * 1024 * 1024
        ),
    )(
        *(pltpu.with_memory_space_constraint(x, pltpu.HBM) for x in operands),
    )
    return tuple(
        pl.pallas_call(
            store,
            out_shape=tuple(pltpu.HBM(x.shape, x.dtype) for x in held),
            in_specs=[vmem, vmem],
            out_specs=(hbm, hbm),
            scratch_shapes=[dma((2,))],
        )(*(pltpu.with_memory_space_constraint(x, pltpu.VMEM) for x in held))
    )


def solution(mesh):
    in_specs = (
        P("group", None),
        P(None, "group", "head"),
        P(),
        P(("head", "group"), None),
        P(),
        P("group", "head"),
        P("group", "head"),
        P("group", "head"),
        P(),
        P("group", "head"),
        P(),
        P("group", "head"),
    )
    out_specs = (P("group", "head"), P("group", None))
    step = functools.partial(shards, mesh.shape["group"], mesh.shape["head"])
    return jax.shard_map(step, mesh=mesh, in_specs=in_specs, out_specs=out_specs, check_vma=False)
```

```python
import functools
import math

import jax
import jax.numpy as jnp
from jax import lax
from jax.experimental import pallas as pl
from jax.experimental.pallas import tpu as pltpu
from jax.sharding import PartitionSpec as P

MESH = pl.DeviceIdType.MESH
BF16 = jnp.bfloat16
F32 = jnp.float32
DK = 128
LANES = 128
EPS = 1e-06


def mm(a, b, ca, cb):
    return lax.dot_general(a, b, (((ca,), (cb,)), ((), ())), preferred_element_type=F32)


def kernel(
    ngroup,
    nhead,
    mem,
    sources_hbm,
    keep_hbm,
    resid_hbm,
    qkv_hbm,
    enc_bias_hbm,
    gain_hbm,
    cross_bias_hbm,
    out_w,
    key_w,
    value_w,
    query_hbm,
    grad_hbm,
    context,
    memory_grad,
    sources,
    keep,
    resid,
    qkv,
    enc_bias,
    gain,
    cross_bias,
    wo,
    kw,
    vw,
    query,
    grad,
    flat,
    resid_flat,
    out_send,
    out_recv,
    norm_all,
    norm_pick,
    dn_send,
    dn_near,
    dn_sum,
    dn_far,
    probs,
    pick,
    dn_out,
    dn_in,
    mg_all,
    local_sem,
    wo_send,
    wo_recv,
    wo_pass_send,
    wo_pass_recv,
    kv_send,
    kv_recv,
    kv_pass_send,
    kv_pass_recv,
    far_recv,
    near_recv,
    phase_send,
    phase_recv,
    ready,
):
    seq, dim = resid.shape
    width = query.shape[1]
    nheads = width // DK
    chunks = dim // LANES
    own_rows = seq // nhead
    blk = own_rows * chunks
    scale = 1.0 / math.sqrt(DK)
    g = lax.axis_index("group")
    h = lax.axis_index("head")
    core = lax.rem(g, 2)
    chip = lax.div(g, 2)
    sibling = g + 1 - 2 * core
    nchip = ngroup // 2

    nz, nx = nhead // 2, ngroup // 4
    z, y = lax.div(h, 2), lax.rem(h, 2)
    gx, gy = lax.div(g, 4), lax.rem(lax.div(g, 2), 2)

    def each(n, body):
        lax.fori_loop(1, n, lambda k, c: (body(k), c)[1], 0)

    def head_at(dz, dy):
        return lax.rem(z + dz + nz, nz) * 2 + lax.rem(y + dy, 2)

    def group_at(dx, dy, dc):
        return lax.rem(gx + dx, nx) * 4 + lax.rem(gy + dy, 2) * 2 + lax.rem(core + dc, 2)

    head_steps = sorted(
        [(dz, dy) for dz in range(nz) for dy in range(2)][1:], key=lambda t: -(min(t[0], nz - t[0]) * 2 + t[1])
    )

    def head_peer(k):
        j = lax.div(k - 1, 2)
        away = nz // 2 - lax.div(j + 1, 2)
        return head_at(away * (2 * lax.rem(j, 2) - 1), lax.rem(k, 2))

    def spread(dx, dy, dc):
        return -(min(dx, nx - dx) * 4 + dy * 4 + dc)

    steps = [(dx, dy, dc) for dx in range(nx) for dy in range(2) for dc in range(2)][1:]
    group_steps = sorted(steps, key=lambda t: spread(*t))
    chip_steps = [(dx, dy) for dx, dy, dc in group_steps if dc == 0]
    far_steps = sorted(range(2, nz, 4), key=lambda a: -min(a, nz - a))
    near_steps = [(2, 1), (1, 1), (nz - 1, 1), (0, 1), (2, 0), (1, 0), (nz - 1, 0)]

    def remote(src, dst, send, recv, where):
        return pltpu.make_async_remote_copy(
            src_ref=src,
            dst_ref=dst,
            send_sem=send,
            recv_sem=recv,
            device_id=where,
            device_id_type=MESH,
        )

    def total(ref, send, recv):
        return remote(ref, ref, send, recv, {"group": sibling})

    barrier = pltpu.get_barrier_semaphore()
    even, odd = g - core, g - core + 1

    def hello(**where):
        pl.semaphore_signal(barrier, inc=1, device_id=where, device_id_type=MESH)

    def tell_sibling():
        pl.semaphore_signal(ready, inc=1, device_id={"group": sibling}, device_id_type=MESH)

    for step in chip_steps:
        hello(group=group_at(*step, 0) - core)
    pl.when(core == 1)(lambda: hello(group=even))
    for step in head_steps:
        hello(group=odd, head=head_at(*step))
    locals_ = [
        pltpu.make_async_copy(query_hbm, query, local_sem.at[0]),
        pltpu.make_async_copy(grad_hbm, grad, local_sem.at[1]),
        pltpu.make_async_copy(out_w, wo.at[g], local_sem.at[2]),
        pltpu.make_async_copy(key_w, kw.at[g], local_sem.at[3]),
        pltpu.make_async_copy(value_w, vw.at[g], local_sem.at[4]),
        pltpu.make_async_copy(qkv_hbm, qkv, local_sem.at[5]),
        pltpu.make_async_copy(enc_bias_hbm, enc_bias, local_sem.at[6]),
        pltpu.make_async_copy(resid_hbm, resid, local_sem.at[7]),
        pltpu.make_async_copy(gain_hbm, gain, local_sem.at[8]),
        pltpu.make_async_copy(cross_bias_hbm, cross_bias, local_sem.at[9]),
        pltpu.make_async_copy(sources_hbm, sources, local_sem.at[10]),
        pltpu.make_async_copy(keep_hbm, keep, local_sem.at[11]),
    ]
    for copy in locals_:
        copy.start()

    @pl.when(core == 0)
    def _():
        pl.semaphore_wait(barrier, ngroup - 1)
        tell_sibling()

    @pl.when(core == 1)
    def _():
        pl.semaphore_wait(ready, 1)

    locals_[2].wait()
    for i, (dx, dy) in enumerate(chip_steps):
        remote(wo.at[g], wo.at[g], wo_send, wo_recv.at[i], {"group": group_at(dx, dy, 0)}).start()
    remote(wo.at[g], wo.at[g], wo_pass_send, wo_pass_recv, {"group": sibling}).start()

    locals_[3].wait()
    locals_[4].wait()
    locals_[5].wait()
    locals_[6].wait()
    bias = enc_bias[...]
    ctx = []
    for n in range(nheads):
        cols = slice(n * DK, (n + 1) * DK)
        scores = mm(qkv[0, :, cols], qkv[1, :, cols], 1, 1) * scale + bias
        e = jnp.exp(scores - jnp.max(scores, axis=1, keepdims=True))
        p = (e * (1.0 / jnp.sum(e, axis=1, keepdims=True))).astype(BF16)
        ctx.append(mm(p, qkv[2, :, cols], 1, 0).astype(BF16))
    ctx = jnp.concatenate(ctx, axis=1)

    def to_flat(x, ref, base):
        rows = x.shape[0]
        for c in range(chunks):
            ref[pl.ds(base * chunks + c, rows, stride=chunks), :] = x[:, c * LANES : (c + 1) * LANES]

    def from_flat(ref, base, rows, c):
        return ref[pl.ds(base * chunks + c, rows, stride=chunks), :]

    locals_[7].wait()
    to_flat(resid[...].astype(F32), resid_flat, 0)

    locals_[10].wait()
    for e in range(ngroup):
        for s in range(mem):
            reads = (sources[s, g] == e).astype(jnp.int32)
            pick[e * mem + s] = jnp.full((blk, LANES), reads, jnp.int32).astype(F32)

    for i, (dx, dy) in enumerate(chip_steps):
        there = wo.at[group_at(nx - dx, dy, 0)]
        remote(there, there, wo_send, wo_recv.at[i], {"group": sibling}).wait_recv()
        remote(there, there, wo_pass_send, wo_pass_recv, {"group": sibling}).start()

    @pl.when(core == 1)
    def _():
        pl.semaphore_wait(barrier, 2 * (nhead - 1))
        tell_sibling()

    total(wo.at[pl.ds(0, nchip)], wo_pass_send, wo_pass_recv).wait_recv()
    part = mm(ctx, wo[...].reshape(width, dim), 1, 0)

    to_flat(part, flat, 0)
    out_send[...] = flat[pl.ds(0, seq * chunks), :].reshape(nhead, blk, LANES).astype(BF16)

    @pl.when(core == 0)
    def _():
        pl.semaphore_wait(ready, 1)

    for i, step in enumerate(head_steps):
        there = head_at(*step)
        remote(out_send.at[there], out_recv.at[i], phase_send.at[0], phase_recv.at[0], {"head": there}).start()

    across = chip_steps.index((0, 1))
    along = [(i, dx) for i, (dx, dy) in enumerate(chip_steps) if dy == 0]

    def send_weight(j, ref):
        there = ref.at[g]
        remote(there, there, kv_send, kv_recv.at[j, across], {"group": group_at(0, 1, 0)}).start()
        for i, dx in along:
            remote(there, there, kv_send, kv_recv.at[j, i], {"group": group_at(dx, 0, 0)}).start()
        remote(there, there, kv_pass_send, kv_pass_recv.at[j], {"group": sibling}).start()

    def relay_weight(j, ref):
        there = ref.at[group_at(0, 1, 0)]
        remote(there, there, kv_send, kv_recv.at[j, across], {"group": sibling}).wait_recv()
        for _, dx in along:
            i = chip_steps.index((dx, 1))
            remote(there, there, kv_send, kv_recv.at[j, i], {"group": group_at(dx, 0, 0)}).start()
        remote(there, there, kv_pass_send, kv_pass_recv.at[j], {"group": sibling}).start()

    def pass_kv(j, ref):
        for i, (dx, dy) in enumerate(chip_steps):
            if i == across:
                continue
            there = ref.at[group_at(nx - dx, dy, 0)]
            remote(there, there, kv_send, kv_recv.at[j, i], {"group": sibling}).wait_recv()
            remote(there, there, kv_pass_send, kv_pass_recv.at[j], {"group": sibling}).start()

    send_weight(0, kw)
    relay_weight(0, kw)

    mine = pl.ds(pl.multiple_of(h * blk, blk), blk)
    memory = flat[mine, :] + resid_flat[mine, :]
    total(out_recv, phase_send.at[0], phase_recv.at[0]).wait_recv()
    memory = memory + jnp.sum(out_recv[...].astype(F32), axis=0)

    def row_mean(x):
        x3 = x.reshape(own_rows, chunks, LANES)
        m = jnp.sum(jnp.sum(x3, axis=1, keepdims=True), axis=2, keepdims=True) * (1.0 / dim)
        return jnp.broadcast_to(m, x3.shape).reshape(blk, LANES)

    locals_[8].wait()
    gains = jnp.broadcast_to(gain[...][None], (own_rows, chunks, LANES)).reshape(blk, LANES)
    inv = lax.rsqrt(row_mean(memory * memory) + EPS)
    normed = memory * inv
    norm_all[g] = (normed * gains).astype(BF16)

    there = norm_all.at[g]
    for step in group_steps:
        remote(there, there, phase_send.at[1], phase_recv.at[1], {"group": group_at(*step)}).start()
    pass_kv(0, kw)
    total(norm_all.at[pl.ds(0, ngroup - 1)], phase_send.at[1], phase_recv.at[1]).wait_recv()

    for s in range(mem):
        norm_pick[h, s * blk : (s + 1) * blk, :] = norm_all[sources[s, g]]

    there = norm_pick.at[h]
    for i, a in enumerate(far_steps):
        remote(there, there, phase_send.at[2], far_recv.at[i], {"head": head_at(a, 0)}).start()
    send_weight(1, vw)

    relay_weight(1, vw)

    nfar = len(far_steps)
    npass = nfar * len(near_steps) - 1
    for i, a in reversed(list(enumerate(far_steps))):
        there = norm_pick.at[head_at(nz - a, 0)]
        remote(there, there, phase_send.at[2], far_recv.at[i], {"head": head_at(a, 0)}).wait_recv()
        for b, dy in near_steps:
            if (a + b) % nz or dy:
                remote(there, there, phase_send.at[6], phase_recv.at[2], {"head": head_at(b, dy)}).start()
    pass_kv(1, vw)
    for i in (0, 9, 11):
        locals_[i].wait()
    total(kw.at[pl.ds(0, nchip)], kv_pass_send, kv_pass_recv.at[0]).wait_recv()
    total(norm_pick.at[pl.ds(0, npass)], phase_send.at[6], phase_recv.at[2]).wait_recv()
    for s in range(mem):
        rows = norm_pick[:, s * blk : (s + 1) * blk, :].astype(F32).reshape(seq * chunks, LANES)
        flat[pl.ds(s * seq * chunks, seq * chunks), :] = rows
    rows = mem * seq
    picked = jnp.concatenate([from_flat(flat, 0, rows, c).astype(BF16) for c in range(chunks)], axis=1)

    key_full = kw[...].reshape(dim, width)
    keys = mm(picked, key_full, 1, 0).astype(BF16)
    cbias = cross_bias[...]
    qrows = query.shape[0]
    for n in range(nheads):
        cols = slice(n * DK, (n + 1) * DK)
        cross = (mm(keys[:, cols], query[:, cols], 1, 1) * scale).reshape(mem, seq, qrows) + cbias[None]
        cross = cross.reshape(rows, qrows)
        e = jnp.exp(cross - jnp.max(cross, axis=0, keepdims=True))
        probs[n] = e * (1.0 / jnp.sum(e, axis=0, keepdims=True))

    locals_[1].wait()
    total(vw.at[pl.ds(0, nchip)], kv_pass_send, kv_pass_recv.at[1]).wait_recv()
    value_full = vw[...].reshape(dim, width)
    values = mm(picked, value_full, 1, 0).astype(BF16)
    dks, dvs = [], []
    for n in range(nheads):
        cols = slice(n * DK, (n + 1) * DK)
        kept = keep[0, n].astype(F32)
        q_n, g_n, v_n = query[:, cols], grad[:, cols], values[:, cols]
        prob = probs[n]
        prob_low = prob.astype(BF16)
        context[:, cols] = (mm(prob_low, v_n, 0, 0) * kept).astype(BF16)
        dprob = mm(v_n, g_n, 1, 1)
        delta = jnp.sum(prob * dprob, axis=0, keepdims=True)
        dscore = (prob * (dprob - delta) * (scale * kept)).astype(BF16)
        dks.append(mm(dscore, q_n, 1, 0).astype(BF16))
        dvs.append((mm(prob_low, g_n, 1, 0) * kept).astype(BF16))
    dks = jnp.concatenate(dks, axis=1)
    dvs = jnp.concatenate(dvs, axis=1)
    dnorm = mm(dks, key_full, 1, 1) + mm(dvs, value_full, 1, 1)

    to_flat(dnorm, flat, 0)
    for s in range(mem):
        block = flat[pl.ds(s * seq * chunks, seq * chunks), :].reshape(nhead, blk, LANES)
        dn_send[:, s * blk : (s + 1) * blk, :] = block.astype(BF16)

    for i, a in enumerate(far_steps):
        for j, (b, dy) in enumerate(near_steps):
            there = dn_send.at[head_at(a + b, dy)]
            remote(there, dn_near.at[i, j], phase_send.at[3], near_recv.at[i], {"head": head_at(b, dy)}).start()
    for i, a in enumerate(far_steps):
        total(dn_near.at[i], phase_send.at[3], near_recv.at[i]).wait_recv()
        near = dn_send[head_at(a, 0)].astype(F32) + jnp.sum(dn_near[i].astype(F32), axis=0)
        dn_sum[i] = near.astype(BF16)
        remote(dn_sum.at[i], dn_far.at[i], phase_send.at[7], phase_recv.at[3], {"head": head_at(a, 0)}).start()
    total(dn_far, phase_send.at[7], phase_recv.at[3]).wait_recv()
    dn_sum_all = jnp.sum(dn_far[...].astype(F32), axis=0)

    for e in range(ngroup):
        acc = jnp.zeros((blk, LANES), F32)
        for s in range(mem):
            acc = acc + dn_sum_all[s * blk : (s + 1) * blk] * pick[e * mem + s]
        dn_out[e] = acc.astype(BF16)
    for i, step in enumerate(group_steps):
        there = group_at(*step)
        remote(dn_out.at[there], dn_in.at[i], phase_send.at[4], phase_recv.at[4], {"group": there}).start()
    acc = dn_out[g].astype(F32)
    total(dn_in, phase_send.at[4], phase_recv.at[4]).wait_recv()
    acc = acc + jnp.sum(dn_in[...].astype(F32), axis=0)
    scaled = acc * gains
    mg_all[h] = (inv * (scaled - normed * row_mean(scaled * normed))).astype(BF16)

    there = mg_all.at[h]
    for step in head_steps:
        remote(there, there, phase_send.at[5], phase_recv.at[5], {"head": head_at(*step)}).start()
    total(mg_all.at[pl.ds(0, nhead - 1)], phase_send.at[5], phase_recv.at[5]).wait_recv()
    flat[pl.ds(0, seq * chunks), :] = mg_all[...].astype(F32).reshape(seq * chunks, LANES)
    for c in range(chunks):
        memory_grad[:, c * LANES : (c + 1) * LANES] = from_flat(flat, 0, seq, c).astype(BF16)

    total(wo.at[pl.ds(0, nchip - 1)], wo_send, wo_recv.at[0]).wait_send()
    total(wo.at[pl.ds(0, nchip)], wo_pass_send, wo_pass_recv).wait_send()
    total(kw.at[pl.ds(0, 2 * nchip - 2)], kv_send, kv_recv.at[0, 0]).wait_send()
    total(kw.at[pl.ds(0, 2 * nchip)], kv_pass_send, kv_pass_recv.at[0]).wait_send()
    sent = (
        out_recv,
        norm_all.at[pl.ds(0, ngroup - 1)],
        norm_pick.at[pl.ds(0, nfar)],
        dn_near,
        dn_in,
        mg_all.at[pl.ds(0, nhead - 1)],
        norm_pick.at[pl.ds(0, npass)],
        dn_far,
    )
    for i, ref in enumerate(sent):
        total(ref, phase_send.at[i], phase_recv.at[0]).wait_send()


def store(context, memory_grad, context_hbm, memory_grad_hbm, sem):
    copies = (
        pltpu.make_async_copy(context, context_hbm, sem.at[0]),
        pltpu.make_async_copy(memory_grad, memory_grad_hbm, sem.at[1]),
    )
    for copy in copies:
        copy.start()
    for copy in copies:
        copy.wait()


def shards(
    ngroup,
    nhead,
    enc_resid,
    enc_qkv,
    enc_bias,
    out_weight,
    final_gain,
    key_weight,
    value_weight,
    dec_query,
    cross_bias,
    out_grad,
    sources,
    head_keep,
):
    seq, dim = enc_resid.shape
    qrows, width = dec_query.shape
    mem = sources.shape[1]
    chunks = dim // LANES
    blk = seq // nhead * chunks
    nchip = ngroup // 2
    nfar = nhead // 8
    vmem = pl.BlockSpec(memory_space=pltpu.VMEM)
    hbm = pl.BlockSpec(memory_space=pltpu.HBM)
    dma = pltpu.SemaphoreType.DMA
    operands = (
        sources.T,
        head_keep,
        enc_resid,
        enc_qkv,
        enc_bias,
        final_gain.reshape(chunks, LANES),
        cross_bias.T,
        out_weight,
        key_weight,
        value_weight,
        dec_query,
        out_grad,
    )
    held = pl.pallas_call(
        functools.partial(kernel, ngroup, nhead, mem),
        out_shape=(
            pltpu.VMEM((qrows, width), BF16),
            pltpu.VMEM((seq, dim), BF16),
        ),
        in_specs=[hbm] * 12,
        out_specs=(vmem, vmem),
        scratch_shapes=[
            pltpu.SMEM(sources.shape[::-1], jnp.int32),
            pltpu.SMEM(head_keep.shape, jnp.int32),
            pltpu.VMEM(enc_resid.shape, BF16),
            pltpu.VMEM(enc_qkv.shape, BF16),
            pltpu.VMEM(enc_bias.shape, F32),
            pltpu.VMEM((chunks, LANES), F32),
            pltpu.VMEM(cross_bias.shape[::-1], F32),
            pltpu.VMEM((ngroup,) + out_weight.shape, BF16),
            pltpu.VMEM((ngroup,) + key_weight.shape, BF16),
            pltpu.VMEM((ngroup,) + value_weight.shape, BF16),
            pltpu.VMEM((qrows, width), BF16),
            pltpu.VMEM((qrows, width), BF16),
            pltpu.VMEM((mem * seq * chunks, LANES), F32),
            pltpu.VMEM((seq * chunks, LANES), F32),
            pltpu.VMEM((nhead, blk, LANES), BF16),
            pltpu.VMEM((nhead - 1, blk, LANES), BF16),
            pltpu.VMEM((ngroup, blk, LANES), BF16),
            pltpu.VMEM((nhead, mem * blk, LANES), BF16),
            pltpu.VMEM((nhead, mem * blk, LANES), BF16),
            pltpu.VMEM((nfar, 7, mem * blk, LANES), BF16),
            pltpu.VMEM((nfar, mem * blk, LANES), BF16),
            pltpu.VMEM((nfar, mem * blk, LANES), BF16),
            pltpu.VMEM((width // DK, mem * seq, qrows), F32),
            pltpu.VMEM((ngroup * mem, blk, LANES), F32),
            pltpu.VMEM((ngroup, blk, LANES), BF16),
            pltpu.VMEM((ngroup - 1, blk, LANES), BF16),
            pltpu.VMEM((nhead, blk, LANES), BF16),
            dma((12,)),
            dma,
            dma((nchip,)),
            dma,
            dma,
            dma,
            dma((2, nchip)),
            dma,
            dma((2,)),
            dma((nfar,)),
            dma((nfar,)),
            dma((8,)),
            dma((6,)),
            pltpu.SemaphoreType.REGULAR,
        ],
        compiler_params=pltpu.CompilerParams(
            collective_id=0, has_side_effects=True, vmem_limit_bytes=40 * 1024 * 1024
        ),
    )(
        *(pltpu.with_memory_space_constraint(x, pltpu.HBM) for x in operands),
    )
    return tuple(
        pl.pallas_call(
            store,
            out_shape=tuple(pltpu.HBM(x.shape, x.dtype) for x in held),
            in_specs=[vmem, vmem],
            out_specs=(hbm, hbm),
            scratch_shapes=[dma((2,))],
        )(*(pltpu.with_memory_space_constraint(x, pltpu.VMEM) for x in held))
    )


def solution(mesh):
    in_specs = (
        P("group", None),
        P(None, "group", "head"),
        P(),
        P(("head", "group"), None),
        P(),
        P("group", "head"),
        P("group", "head"),
        P("group", "head"),
        P(),
        P("group", "head"),
        P(),
        P("group", "head"),
    )
    out_specs = (P("group", "head"), P("group", None))
    step = functools.partial(shards, mesh.shape["group"], mesh.shape["head"])
    return jax.shard_map(step, mesh=mesh, in_specs=in_specs, out_specs=out_specs, check_vma=False)
```
